128 devices in a mesh: dp: 128 (over z, y, x, core).
Axes of the slice: x: 4, y: 4, z: 4, core: 2. Of those that a mesh axis runs over, the one named last changes fastest.
Arguments:
- text_states: bfloat16 [2048, 16, 768], P('dp'), may hold values from -6 to 6
- text_len: int32 [2048], P('dp'), may hold values from 1 to 16
- query_states: bfloat16 [2048, 16, 768], P('dp'), may hold values from -6 to 6
- neg_owner: int32 [2048, 2], P('dp'), may hold values from 0 to 127, all different within a row; in each aligned block of 16 rows (0 to 15, 16 to 31, ...) at most 2 rows name the same one
- neg_slot: int32 [2048, 2], P('dp'), may hold values from 0 to 15
- projection_weight: bfloat16 [768, 2304], replicated, may hold values from -0.21875 to 0.21875
- output_weight: bfloat16 [768, 768], replicated, may hold values from -0.21875 to 0.21875
- ln_gain: float32 [768], replicated, may hold values from 0.5 to 1.5
- ln_bias: float32 [768], replicated, may hold values from -3 to 3
- itm_weight: float32 [768, 2], replicated, may hold values from -0.875 to 0.875
- itm_bias: float32 [2], replicated, may hold values from -3 to 3
Outputs:
- pair_logits: float32 [2048, 3, 2], P('dp')
- grad_text: bfloat16 [2048, 16, 768], P('dp')
- grad_query: bfloat16 [2048, 16, 768], P('dp')
- grad_qkv: float32 [768, 2304], replicated
- grad_out: float32 [768, 768], replicated
The draws below stay inside these ranges and needn't reach their ends.
Inputs may be any that keep to these rules, and one draw needn't show every extreme that they name: `neg_owner`: the two negatives of a caption lie in different blocks; among the 16 captions of one device no block is named more than 2 times, and in some device exactly 2 times.
All inputs are finite; a program needn't handle non-finite values.
Results may differ from the reference program's by a relative error of at most 0.0075.
Values may be sent and summed in bfloat16 or wider, within the bound.
A program may use at most 128 MiB of HBM per device.

```python
import math
import jax
import jax.numpy as jnp
import numpy as np
from jax import lax

D = 768
HEADS = 12
NQ = 16
L = 16
CAP = 2
P_DEV = 16
CAPTIONS = 2048
N_DP = 128


def touch_ends(result, stream_key, least, top_value):
    longest = result.shape.index(max(result.shape))
    spots = []
    for shift in (0, 1):
        where = [jax.random.randint(jax.random.fold_in(stream_key, axis), (), 0, length) for axis, length in enumerate(result.shape)]
        where[longest] = (where[longest] + shift) % result.shape[longest]
        spots.append(tuple(where))
    return result.at[spots[0]].set(least).at[spots[1]].set(top_value)


def levels(stream_key, extent, shards, least, top_value):
    def one(axis_at, blocks):
        steps = jax.random.uniform(jax.random.fold_in(jax.random.fold_in(stream_key, 6), axis_at), (blocks,), jnp.float32, least / len(shards), top_value / len(shards))
        return jnp.repeat(jnp.exp(steps), extent[axis_at] // blocks).reshape((-1,) + (1,) * (len(extent) - axis_at - 1))

    level = one(*shards[0])
    for cut in shards[1:]:
        level = level * one(*cut)
    return level


def shared_out(own_key, own, number, rows, amount, top, limit, lean):
    ranking = jax.random.permutation(own_key, amount)
    crowded, ordinary = load_shares(amount, rows * top, limit, lean, True), load_shares(amount, rows * top, limit, lean, False)
    places = jnp.arange(amount)

    def named(sizes, offset_by):
        used = int((sizes > 0).sum())
        fixed = max(1, used // 4)
        passed = fixed + (places - fixed + offset_by * (used - fixed)) % max(1, amount - fixed)
        return jnp.zeros((amount,), jnp.int32).at[ranking[jnp.where(places < fixed, places, passed)]].set(jnp.asarray(sizes, jnp.int32))

    sizes = jnp.where(number % 4 == 0, named(crowded, number // 4), named(ordinary, number - number // 4 - 1))
    mixed = jax.random.permutation(jax.random.fold_in(own, 3), amount)
    giver, receiver = mixed[0:amount // 2 * 2:2], mixed[1:amount // 2 * 2:2]
    margin = jnp.minimum(sizes[giver] - 1, limit - sizes[receiver]) // 2
    margin = jnp.where((giver == ranking[0]) | (receiver == ranking[0]) | (sizes[receiver] == 0), 0, jnp.maximum(margin, 0))
    passed = jax.random.randint(jax.random.fold_in(own, 4), (amount // 2,), 0, 1 << 20) % (margin + 1)
    sizes = sizes.at[giver].add(-passed).at[receiver].add(passed)
    items = jnp.searchsorted(jnp.cumsum(sizes), jnp.arange(rows * top), side="right").astype(jnp.int32)
    grid = items.reshape(top, rows).T
    grid = grid[jax.random.permutation(jax.random.fold_in(own, 1), rows)]
    offset_by = jax.random.randint(jax.random.fold_in(own, 2), (rows, 1), 0, top)
    return jnp.take_along_axis(grid, (jnp.arange(top)[None, :] + offset_by) % top, axis=1)


def load_shares(number_of, total, most, slope, full):
    weights = [(1 << 20) // math.isqrt(rank ** slope) + 1 for rank in range(1, number_of + 1)]
    largest = most if full else min(most, max(-(-total // number_of), total * weights[0] // sum(weights)))
    least = 1 if total - largest >= number_of - 1 else 0
    holding, spare = [largest] + [least] * (number_of - 1), total - largest - least * (number_of - 1)
    while spare > 0:
        free = [i for i in range(1, number_of) if holding[i] < largest] or [i for i in range(1, number_of) if holding[i] < most]
        pool, budget = sum([weights[i] for i in free]), spare
        for i in free:
            extra = min(most - holding[i], max(1, budget * weights[i] // pool), spare)
            holding[i] = holding[i] + extra
            spare = spare - extra
    return np.array(holding)


def gaussian(stream_key, shape, scale, most, cuts=(), kind=jnp.bfloat16):
    entries = jax.random.normal(stream_key, shape, jnp.float32) * scale
    if len(cuts) > 0:
        entries = levels(stream_key, shape, cuts, -0.22, 0.18) * entries
    return jnp.clip(entries, min=-most, max=most).astype(kind)


def setup_inputs(seed: int = 0) -> dict:
    arg_keys = jax.random.split(jax.random.key(seed), 12)
    text_states = gaussian(arg_keys[0], (CAPTIONS, L, D), 1.0, 6.0, ((0, 128),))
    text_len = touch_ends(jax.random.randint(arg_keys[1], (CAPTIONS,), 1, L + 1), jax.random.fold_in(arg_keys[1], 1), 1, L).astype(jnp.int32)
    query_states = gaussian(arg_keys[2], (CAPTIONS, NQ, D), 1.0, 6.0, ((0, 128),))
    neg_owner_keys = jax.random.split(jax.random.fold_in(arg_keys[3], 1), CAPTIONS // P_DEV)
    neg_owner_turns = jax.random.permutation(jax.random.fold_in(arg_keys[3], 3), CAPTIONS // P_DEV)
    neg_owner = jax.vmap(lambda own, number: shared_out(jax.random.fold_in(arg_keys[3], 2), own, number, P_DEV, N_DP, 2, CAP, 2))(neg_owner_keys, neg_owner_turns).reshape((CAPTIONS, 2))
    neg_slot = touch_ends(jax.random.randint(arg_keys[4], (CAPTIONS, 2), 0, P_DEV), jax.random.fold_in(arg_keys[4], 1), 0, P_DEV - 1).astype(jnp.int32)
    projection_weight = gaussian(arg_keys[5], (D, 3 * D), D ** -0.5, 0.21875)
    output_weight = gaussian(arg_keys[6], (D, D), D ** -0.5, 0.21875)
    ln_gain = jnp.clip(1.0 + 0.1 * jax.random.normal(arg_keys[7], (D,), jnp.float32), 0.5, 1.5)
    ln_bias = gaussian(arg_keys[8], (D,), 0.5, 3.0, (), jnp.float32)
    itm_weight = gaussian(arg_keys[9], (D, 2), (D // 16) ** -0.5, 0.875, (), jnp.float32)
    itm_bias = gaussian(arg_keys[10], (2,), 1.0, 3.0, (), jnp.float32)
    return dict(text_states=text_states, text_len=text_len, query_states=query_states, neg_owner=neg_owner, neg_slot=neg_slot, projection_weight=projection_weight, output_weight=output_weight, ln_gain=ln_gain, ln_bias=ln_bias, itm_weight=itm_weight, itm_bias=itm_bias)


def matrix_product(einsum_form, left_side, right_side):
    return jnp.einsum(einsum_form, left_side.astype(jnp.float32), right_side.astype(jnp.float32), precision=lax.Precision.HIGHEST)

def split_heads(tensor, head_number):
    return tensor.reshape(tensor.shape[:-1] + (head_number, tensor.shape[-1] // head_number))

def merge_heads(tensor):
    return tensor.reshape(tensor.shape[0], tensor.shape[1], tensor.shape[2] * tensor.shape[3])

def tail_loss(hidden_states, ln_gain, ln_bias, itm_weight, itm_bias, labels):
    center = hidden_states - lax.optimization_barrier(jnp.mean(hidden_states, axis=-1, keepdims=True))
    spread = lax.optimization_barrier(jnp.mean(center * center, axis=-1, keepdims=True))
    normed = center * lax.rsqrt(spread + 1e-06) * ln_gain + ln_bias
    pooled = lax.optimization_barrier(jnp.mean(normed, axis=1))
    logits = jnp.dot(pooled, itm_weight, precision=lax.Precision.HIGHEST) + itm_bias
    losses = jax.nn.logsumexp(logits, axis=-1) - lax.optimization_barrier(jnp.sum(logits * labels, axis=-1))
    return (jnp.sum(losses), logits)

def pair_work(caption_rows, lengths, images, projection_weight, output_weight, ln_gain, ln_bias, itm_weight, itm_bias):
    caption_texts, text_rows, hidden_width = caption_rows.shape
    query_row_count = images.shape[2]
    pair_rows = caption_texts * 3
    head_number = HEADS
    score_scale = 1.0 / math.sqrt(hidden_width // head_number)
    text_kv = matrix_product('bld,de->ble', caption_rows, projection_weight[:, hidden_width:]).astype(jnp.bfloat16)
    image_row_count = images.reshape(pair_rows, query_row_count, hidden_width)
    image_projected = matrix_product('tns,sm->tnm', image_row_count, projection_weight).astype(jnp.bfloat16)
    text_wide = jnp.broadcast_to(text_kv[:, None], (caption_texts, 3, text_rows, 2 * hidden_width)).reshape(pair_rows, text_rows, 2 * hidden_width)
    queries = split_heads(image_projected[:, :, :hidden_width], head_number)
    key_heads = split_heads(jnp.concatenate([image_projected[:, :, hidden_width:2 * hidden_width], text_wide[:, :, :hidden_width]], axis=1), head_number)
    value_heads = split_heads(jnp.concatenate([image_projected[:, :, 2 * hidden_width:], text_wide[:, :, hidden_width:]], axis=1), head_number)
    position = jnp.arange(query_row_count + text_rows)
    key_valid = (position[None, :] < query_row_count) | (position[None, :] - query_row_count < lengths[:, None])
    key_valid = jnp.repeat(key_valid, 3, axis=0)
    scores = matrix_product('bqhe,bkhe->bhqk', queries, key_heads) * score_scale
    scores = jnp.where(key_valid[:, None, None, :], scores, -1e+30)
    shifted = jnp.exp(scores - lax.optimization_barrier(jnp.max(scores, axis=-1, keepdims=True)))
    weights = shifted / lax.optimization_barrier(jnp.sum(shifted, axis=-1, keepdims=True))
    weights_low = weights.astype(jnp.bfloat16)
    attended_context = merge_heads(matrix_product('bhqk,bkhe->bqhe', weights_low, value_heads).astype(jnp.bfloat16))
    hidden_states = image_row_count.astype(jnp.float32) + matrix_product('tns,sm->tnm', attended_context, output_weight)
    labels = jnp.tile(jnp.array([[0.0, 1.0], [1.0, 0.0], [1.0, 0.0]], dtype=jnp.float32), (caption_texts, 1))

    def loss_of(hidden_in):
        return tail_loss(hidden_in, ln_gain, ln_bias, itm_weight, itm_bias, labels)
    loss_total, pullback, logits = jax.vjp(loss_of, hidden_states, has_aux=True)
    hidden_gradient = pullback(jnp.ones_like(loss_total))[0]
    attention_gradient = hidden_gradient.astype(jnp.bfloat16)
    output_weight_gradient = matrix_product('nxv,nxl->vl', attended_context, attention_gradient)
    context_gradient = split_heads(matrix_product('kvp,mp->kvm', attention_gradient, output_weight).astype(jnp.bfloat16), head_number)
    grad_probs = matrix_product('bqhe,bkhe->bhqk', context_gradient, value_heads)
    grad_values = matrix_product('bhqk,bqhe->bkhe', weights_low, context_gradient)
    grad_scores = (weights * (grad_probs - lax.optimization_barrier(jnp.sum(grad_probs * weights, axis=-1, keepdims=True))) * score_scale).astype(jnp.bfloat16)
    grad_queries = merge_heads(matrix_product('bhqk,bkhe->bqhe', grad_scores, key_heads))
    grad_keys = merge_heads(matrix_product('bhqk,bqhe->bkhe', grad_scores, queries))
    grad_values = merge_heads(grad_values)
    image_projection_gradient = jnp.concatenate([grad_queries, grad_keys[:, :query_row_count], grad_values[:, :query_row_count]], axis=-1).astype(jnp.bfloat16)
    grad_text_kv = jnp.concatenate([grad_keys[:, query_row_count:], grad_values[:, query_row_count:]], axis=-1)
    grad_text_kv = lax.optimization_barrier(jnp.sum(grad_text_kv.reshape(caption_texts, 3, text_rows, 2 * hidden_width), axis=1)).astype(jnp.bfloat16)
    image_gradient = (matrix_product('kvp,mp->kvm', image_projection_gradient, projection_weight) + hidden_gradient).reshape(caption_texts, 3, query_row_count, hidden_width)
    grad_text = matrix_product('ble,de->bld', grad_text_kv, projection_weight[:, hidden_width:])
    projection_weight_gradient = matrix_product('nxv,nxl->vl', image_row_count, image_projection_gradient)
    projection_weight_gradient = projection_weight_gradient + jnp.pad(matrix_product('bld,ble->de', caption_rows, grad_text_kv), ((0, 0), (hidden_width, 0)))
    return (logits.reshape(caption_texts, 3, 2), grad_text, image_gradient, projection_weight_gradient, output_weight_gradient)

def reference(text_states, text_len, query_states, neg_owner, neg_slot, projection_weight, output_weight, ln_gain, ln_bias, itm_weight, itm_bias):
    all_pairs = text_states.shape[0]
    hidden_width = text_states.shape[2]
    query_row_count = query_states.shape[1]
    block_rows = math.gcd(all_pairs, 256)
    block_count = all_pairs // block_rows
    neg_image = (neg_owner * P_DEV + neg_slot).astype(jnp.int32)

    def visit_block(state_sum, inputs):
        neg_sum, sum_qkv, sum_out = state_sum
        caption_rows, lengths, own_images, chosen = inputs
        others = jnp.take(query_states, chosen.reshape(-1), axis=0).reshape(block_rows, 2, query_row_count, hidden_width)
        images = jnp.concatenate([own_images[:, None], others], axis=1)
        logits, grad_text, image_gradient, projection_weight_gradient, output_weight_gradient = pair_work(caption_rows, lengths, images, projection_weight, output_weight, ln_gain, ln_bias, itm_weight, itm_bias)
        rounded = lax.optimization_barrier(image_gradient[:, 1:].astype(jnp.bfloat16)).astype(jnp.float32)
        neg_sum = neg_sum.at[chosen.reshape(-1)].add(rounded.reshape(2 * block_rows, query_row_count, hidden_width))
        return ((neg_sum, sum_qkv + projection_weight_gradient, sum_out + output_weight_gradient), (logits, grad_text.astype(jnp.bfloat16), image_gradient[:, 0]))
    initial = (jnp.zeros((all_pairs, query_row_count, hidden_width), jnp.float32), jnp.zeros(projection_weight.shape, jnp.float32), jnp.zeros(output_weight.shape, jnp.float32))
    inputs = (text_states.reshape(block_count, block_rows, text_states.shape[1], hidden_width), text_len.reshape(block_count, block_rows), query_states.reshape(block_count, block_rows, query_row_count, hidden_width), neg_image.reshape(block_count, block_rows, 2))
    finals, stacked = lax.scan(visit_block, initial, inputs)
    neg_sum, sum_qkv, sum_out = finals
    logits, grad_text, grad_own = stacked
    grad_query = (grad_own.reshape(all_pairs, query_row_count, hidden_width) + neg_sum).astype(jnp.bfloat16)
    return (logits.reshape(all_pairs, 3, 2), grad_text.reshape(text_states.shape), grad_query, sum_qkv / all_pairs, sum_out / all_pairs)
```

```python
import math
import jax
import jax.numpy as jnp
from jax import lax
from jax.experimental import pallas as pl
from jax.experimental.pallas import tpu as pltpu
from jax.sharding import PartitionSpec as P

CAP = 2
F32 = jnp.float32
BF = jnp.bfloat16
NN = (((1,), (0,)), ((), ()))
NT = (((1,), (1,)), ((), ()))
TN = (((0,), (0,)), ((), ()))


def mm(a, b, dims):
    return lax.dot_general(a, b, dims, preferred_element_type=F32)


def attention_kernel(
    lens, ibias, x_ref, t_ref, w_ref, wo_ref, gain_ref, bias_ref, iw_ref,
    logits_ref, gtext_ref, own_ref, neg_ref, dw_ref, dwo_ref,
    qkv, tkv, ctx, gh, ga, gc, gqkv, gt, prob,
):
    rows, width = x_ref.shape
    trows = t_ref.shape[0]
    pairs_of_heads = width // 128
    unit = 96
    units = rows // unit
    scale = 1.0 / math.sqrt(64.0)
    col = 256

    def qkv_step(j, _):
        c = pl.ds(pl.multiple_of(j * col, col), col)
        qkv[:, c] = mm(x_ref[...], w_ref[:, c], NN).astype(BF)
        return 0

    lax.fori_loop(0, 3 * width // col, qkv_step, 0)

    def tkv_step(j, _):
        c = pl.ds(pl.multiple_of(j * col, col), col)
        cw = pl.ds(pl.multiple_of(j * col + width, col), col)
        tkv[:, c] = mm(t_ref[...], w_ref[:, cw], NN).astype(BF)
        return 0

    lax.fori_loop(0, 2 * width // col, tkv_step, 0)

    lane = lax.broadcasted_iota(jnp.int32, (1, 128), 1)
    low = lane < 64

    def by_head(a):
        zero = jnp.zeros_like(a)
        return jnp.concatenate([jnp.where(low, a, zero), jnp.where(low, zero, a)], axis=0)

    def keys_of(g, j, first):
        r = pl.ds(pl.multiple_of(g * unit, 32), unit)
        tr = pl.ds(pl.multiple_of(g * 32, 32), 32)
        image = qkv[r, first + j * 128 : first + (j + 1) * 128]
        text = tkv[tr, first - width + j * 128 : first - width + (j + 1) * 128]
        return by_head(jnp.concatenate([image, text], axis=0))

    def forward(g, _):
        r = pl.ds(pl.multiple_of(g * unit, 32), unit)
        rowi = lax.broadcasted_iota(jnp.int32, (unit, 128), 0)
        lanei = lax.broadcasted_iota(jnp.int32, (unit, 128), 1)
        first = rowi < 48
        start = jnp.where(first, 96, 112)
        live = jnp.where(first, lens[2 * g], lens[2 * g + 1])
        block = rowi - lax.rem(rowi, 16)
        valid = ((lanei >= block) & (lanei < block + 16)) | ((lanei >= start) & (lanei < start + live))
        for j in range(pairs_of_heads):
            q = qkv[r, j * 128 : (j + 1) * 128]
            s = mm(q, keys_of(g, j, width), NT) * scale
            parts = []
            for h in range(2):
                sh = jnp.where(valid, s[:, h * 128 : (h + 1) * 128], -1e30)
                e = jnp.exp(sh - jnp.max(sh, axis=-1, keepdims=True))
                parts.append(e / jnp.sum(e, axis=-1, keepdims=True))
            p = jnp.concatenate(parts, axis=1)
            prob[r, j * 256 : (j + 1) * 256] = p
            ctx[r, j * 128 : (j + 1) * 128] = mm(p.astype(BF), keys_of(g, j, 2 * width), NN).astype(BF)
        return 0

    lax.fori_loop(0, units, forward, 0)

    gw0 = gain_ref[...] * iw_ref[0:1, :]
    gw1 = gain_ref[...] * iw_ref[1:2, :]
    slope = (gw1 - gw0) * (1.0 / 16.0)
    slope_mean = jnp.mean(slope)
    base0 = jnp.sum(bias_ref[...] * iw_ref[0:1, :]) + ibias[0]
    base1 = jnp.sum(bias_ref[...] * iw_ref[1:2, :]) + ibias[1]
    part = 192
    tails = part // 16

    def tail(m, _):
        r = pl.ds(pl.multiple_of(m * part, 64), part)
        h = x_ref[r, :].astype(F32) + mm(ctx[r, :], wo_ref[...], NN)
        center = h - jnp.mean(h, axis=-1, keepdims=True)
        spread = jnp.mean(center * center, axis=-1, keepdims=True)
        rstd = lax.rsqrt(spread + 1e-6)
        xhat = center * rstd
        a0 = jnp.sum(xhat * gw0, axis=-1, keepdims=True)
        a1 = jnp.sum(xhat * gw1, axis=-1, keepdims=True)
        l0 = jnp.mean(a0.reshape(tails, 16, 1), axis=1, keepdims=True) + base0
        l1 = jnp.mean(a1.reshape(tails, 16, 1), axis=1, keepdims=True) + base1
        kind = lax.rem(lax.broadcasted_iota(jnp.int32, (tails, 1, 1), 0), 3)
        sign = jnp.where(kind == 0, -1.0, 1.0)
        g1 = sign / (1.0 + jnp.exp(-sign * (l1 - l0)))
        g1 = jnp.broadcast_to(g1, (tails, 16, 1)).reshape(part, 1)
        moved = (a1 - a0) * (1.0 / (16.0 * width))
        g = (rstd * g1) * ((slope - slope_mean) - xhat * moved)
        gh[r, :] = g
        low_g = g.astype(BF)
        ga[r, :] = low_g
        gc[r, :] = mm(low_g, wo_ref[...], NT).astype(BF)
        both = jnp.where(lax.broadcasted_iota(jnp.int32, (tails, 1, 128), 2) == 0, l0, l1)
        logits_ref[pl.ds(m * tails, tails)] = both
        return 0

    lax.fori_loop(0, rows // part, tail, 0)

    def backward(g, _):
        r = pl.ds(pl.multiple_of(g * unit, 32), unit)
        tr = pl.ds(pl.multiple_of(g * 32, 32), 32)
        for j in range(pairs_of_heads):
            c = slice(j * 128, (j + 1) * 128)
            gcj = gc[r, c]
            gp = mm(gcj, keys_of(g, j, 2 * width), NT)
            p = prob[r, j * 256 : (j + 1) * 256]
            gs, pl_low = [], []
            for h in range(2):
                ph = p[:, h * 128 : (h + 1) * 128]
                gph = gp[:, h * 128 : (h + 1) * 128]
                mean = jnp.sum(gph * ph, axis=-1, keepdims=True)
                gs.append((ph * (gph - mean) * scale).astype(BF))
                pl_low.append(ph.astype(BF))
            gq = mm(jnp.concatenate(gs, axis=1), keys_of(g, j, width), NN)
            gk = mm(jnp.concatenate(gs, axis=0), by_head(qkv[r, c]), TN).astype(BF)
            gv = mm(jnp.concatenate(pl_low, axis=0), by_head(gcj), TN).astype(BF)
            gqkv[r, c] = gq.astype(BF)
            gqkv[r, width + j * 128 : width + (j + 1) * 128] = gk[:96]
            gqkv[r, 2 * width + j * 128 : 2 * width + (j + 1) * 128] = gv[:96]
            gt[tr, c] = gk[96:]
            gt[tr, width + j * 128 : width + (j + 1) * 128] = gv[96:]
        return 0

    lax.fori_loop(0, units, backward, 0)

    def to_rows(m, _):
        r = pl.ds(pl.multiple_of(m * part, 64), part)
        g = mm(gqkv[r, :], w_ref[...], NT) + gh[r, :]
        for k in range(part // 48):
            own = pl.ds(pl.multiple_of(m * (part // 3) + k * 16, 16), 16)
            neg = pl.ds(pl.multiple_of(m * (2 * part // 3) + k * 32, 32), 32)
            own_ref[own, :] = g[k * 48 : k * 48 + 16]
            neg_ref[neg, :] = g[k * 48 + 16 : k * 48 + 48].astype(BF)
        return 0

    lax.fori_loop(0, rows // part, to_rows, 0)
    gtext_ref[...] = mm(gt[...], w_ref[:, width:], NT).astype(BF)

    def weight_step(j, _):
        c = pl.ds(pl.multiple_of(j * col, col), col)
        dw_ref[:, c] = mm(x_ref[...], gqkv[:, c], TN)
        return 0

    lax.fori_loop(0, width // col, weight_step, 0)

    def weight_text_step(j, _):
        c = pl.ds(pl.multiple_of(j * col + width, col), col)
        ct = pl.ds(pl.multiple_of(j * col, col), col)
        dw_ref[:, c] = mm(x_ref[...], gqkv[:, c], TN) + mm(t_ref[...], gt[:, ct], TN)
        return 0

    lax.fori_loop(0, 2 * width // col, weight_text_step, 0)

    def out_step(j, _):
        c = pl.ds(pl.multiple_of(j * col, col), col)
        dwo_ref[:, c] = mm(ctx[...], ga[:, c], TN)
        return 0

    lax.fori_loop(0, width // col, out_step, 0)


def attention(images, texts, lens, w, wo, gain, bias, iw, ib):
    rows, width = images.shape
    trows = texts.shape[0]
    vmem = pl.BlockSpec(memory_space=pltpu.VMEM)
    smem = pl.BlockSpec(memory_space=pltpu.SMEM)
    shape = jax.ShapeDtypeStruct
    return pl.pallas_call(
        attention_kernel,
        out_shape=(
            shape((rows // 16, 1, 128), F32),
            shape((trows, width), BF),
            shape((rows // 3, width), F32),
            shape((2 * rows // 3, width), BF),
            shape((width, 3 * width), F32),
            shape((width, width), F32),
        ),
        in_specs=[smem, smem] + [vmem] * 7,
        out_specs=(vmem,) * 6,
        scratch_shapes=[
            pltpu.VMEM((rows, 3 * width), BF),
            pltpu.VMEM((trows, 2 * width), BF),
            pltpu.VMEM((rows, width), BF),
            pltpu.VMEM((rows, width), F32),
            pltpu.VMEM((rows, width), BF),
            pltpu.VMEM((rows, width), BF),
            pltpu.VMEM((rows, 3 * width), BF),
            pltpu.VMEM((trows, 2 * width), BF),
            pltpu.VMEM((rows, 2 * width), F32),
        ],
        compiler_params=pltpu.CompilerParams(vmem_limit_bytes=60 * 1024 * 1024),
        name="pair_attention",
    )(lens, ib, images, texts, w, wo, gain.reshape(1, -1), bias.reshape(1, -1), iw.T)


def on_device(
    text_states, text_len, query_states, neg_owner, neg_slot,
    projection_weight, output_weight, ln_gain, ln_bias, itm_weight, itm_bias,
):
    captions, query_rows, width = query_states.shape
    peers = lax.axis_size("dp")
    requests = captions * CAP
    owner, slot = neg_owner.reshape(-1), neg_slot.reshape(-1)
    ids = jnp.arange(requests)
    rank = jnp.sum(
        ((owner[:, None] == owner[None, :]) & (ids[:, None] > ids[None, :])).astype(jnp.int32), axis=1
    )
    hot = (owner * CAP + rank)[:, None] == jnp.arange(peers * CAP)[None, :]
    wanted = jnp.sum(jnp.where(hot, slot[:, None] + 1, 0), axis=0).reshape(peers, CAP)
    requested = lax.all_to_all(wanted, "dp", split_axis=0, concat_axis=0, tiled=True)
    send = (requested.reshape(-1)[:, None] == jnp.arange(captions)[None, :] + 1).astype(BF)
    flat = query_states.reshape(captions, -1)
    outgoing = jnp.dot(send, flat, preferred_element_type=F32).astype(BF)
    fetched = lax.all_to_all(
        outgoing.reshape(peers, CAP, query_rows, width), "dp", split_axis=0, concat_axis=0, tiled=True
    )
    take = hot.astype(BF)
    negatives = jnp.dot(take, fetched.reshape(peers * CAP, -1), preferred_element_type=F32).astype(BF)
    images = jnp.concatenate(
        [query_states[:, None], negatives.reshape(captions, CAP, query_rows, width)], axis=1
    )
    logits, grad_text, own, back, dw, dwo = attention(
        images.reshape(-1, width), text_states.reshape(-1, width), text_len,
        projection_weight, output_weight, ln_gain, ln_bias, itm_weight, itm_bias,
    )
    outgoing_grads = jnp.dot(take.T, back.reshape(requests, -1), preferred_element_type=F32).astype(BF)
    returned = lax.all_to_all(
        outgoing_grads.reshape(peers, CAP, query_rows, width), "dp", split_axis=0, concat_axis=0, tiled=True
    )
    sum_qkv, sum_out = lax.psum((dw, dwo), "dp")
    received = jnp.dot(send.T, returned.reshape(peers * CAP, -1), preferred_element_type=F32)
    grad_query = (own.reshape(captions, -1) + received).astype(BF).reshape(query_states.shape)
    total = captions * peers
    return (
        logits[:, 0, :2].reshape(captions, 3, 2),
        grad_text.reshape(text_states.shape),
        grad_query,
        sum_qkv / total,
        sum_out / total,
    )


def solution(mesh):
    rows = P("dp", None, None)
    placed = (rows, P("dp"), rows, P("dp", None), P("dp", None)) + (P(),) * 6
    return jax.shard_map(
        on_device, mesh=mesh, in_specs=placed, out_specs=(rows, rows, rows, P(), P()), check_vma=False
    )
```

```python
import math
import jax
import jax.numpy as jnp
from jax import lax
from jax.experimental import pallas as pl
from jax.experimental.pallas import tpu as pltpu
from jax.sharding import PartitionSpec as P

F32 = jnp.float32
BF = jnp.bfloat16
NN = (((1,), (0,)), ((), ()))
NT = (((1,), (1,)), ((), ()))
TN = (((0,), (0,)), ((), ()))


def mm(a, b, dims):
    return lax.dot_general(a, b, dims, preferred_element_type=F32)


def attention_kernel(
    lens, ibias, x_ref, t_ref, w_ref, wo_ref, gain_ref, bias_ref, iw_ref,
    logits_ref, gtext_ref, own_ref, neg_ref, dw_ref,
    qkv, tkv, ctx, gh, ga, gc, gqkv, gt, prob,
):
    rows, width = x_ref.shape
    trows = t_ref.shape[0]
    pairs_of_heads = width // 128
    unit = 96
    units = rows // unit
    scale = 1.0 / math.sqrt(64.0)
    col = 256

    def qkv_step(j, _):
        c = pl.ds(pl.multiple_of(j * col, col), col)
        qkv[:, c] = mm(x_ref[...], w_ref[:, c], NN).astype(BF)
        return 0

    lax.fori_loop(0, 3 * width // col, qkv_step, 0)

    def tkv_step(j, _):
        c = pl.ds(pl.multiple_of(j * col, col), col)
        cw = pl.ds(pl.multiple_of(j * col + width, col), col)
        tkv[:, c] = mm(t_ref[...], w_ref[:, cw], NN).astype(BF)
        return 0

    lax.fori_loop(0, 2 * width // col, tkv_step, 0)

    lane = lax.broadcasted_iota(jnp.int32, (1, 128), 1)
    low = lane < 64

    def by_head(a):
        zero = jnp.zeros_like(a)
        return jnp.concatenate([jnp.where(low, a, zero), jnp.where(low, zero, a)], axis=0)

    def keys_of(g, j, first):
        r = pl.ds(pl.multiple_of(g * unit, 32), unit)
        tr = pl.ds(pl.multiple_of(g * 32, 32), 32)
        image = qkv[r, first + j * 128 : first + (j + 1) * 128]
        text = tkv[tr, first - width + j * 128 : first - width + (j + 1) * 128]
        return by_head(jnp.concatenate([image, text], axis=0))

    def forward(g, _):
        r = pl.ds(pl.multiple_of(g * unit, 32), unit)
        rowi = lax.broadcasted_iota(jnp.int32, (unit, 128), 0)
        lanei = lax.broadcasted_iota(jnp.int32, (unit, 128), 1)
        first = rowi < 48
        start = jnp.where(first, 96, 112)
        live = jnp.where(first, lens[2 * g], lens[2 * g + 1])
        block = rowi - lax.rem(rowi, 16)
        valid = ((lanei >= block) & (lanei < block + 16)) | ((lanei >= start) & (lanei < start + live))
        for j in range(pairs_of_heads):
            q = qkv[r, j * 128 : (j + 1) * 128]
            s = mm(q, keys_of(g, j, width), NT) * scale
            parts = []
            for h in range(2):
                sh = jnp.where(valid, s[:, h * 128 : (h + 1) * 128], -1e30)
                e = jnp.exp(sh - jnp.max(sh, axis=-1, keepdims=True))
                parts.append(e / jnp.sum(e, axis=-1, keepdims=True))
            p = jnp.concatenate(parts, axis=1)
            prob[r, j * 256 : (j + 1) * 256] = p
            ctx[r, j * 128 : (j + 1) * 128] = mm(p.astype(BF), keys_of(g, j, 2 * width), NN).astype(BF)
        return 0

    lax.fori_loop(0, units, forward, 0)

    gw0 = gain_ref[...] * iw_ref[0:1, :]
    gw1 = gain_ref[...] * iw_ref[1:2, :]
    slope = (gw1 - gw0) * (1.0 / 16.0)
    slope_mean = jnp.mean(slope)
    base0 = jnp.sum(bias_ref[...] * iw_ref[0:1, :]) + ibias[0]
    base1 = jnp.sum(bias_ref[...] * iw_ref[1:2, :]) + ibias[1]
    part = 192
    tails = part // 16

    def tail(m, _):
        r = pl.ds(pl.multiple_of(m * part, 64), part)
        h = x_ref[r, :].astype(F32) + mm(ctx[r, :], wo_ref[...], NN)
        center = h - jnp.mean(h, axis=-1, keepdims=True)
        spread = jnp.mean(center * center, axis=-1, keepdims=True)
        rstd = lax.rsqrt(spread + 1e-6)
        xhat = center * rstd
        a0 = jnp.sum(xhat * gw0, axis=-1, keepdims=True)
        a1 = jnp.sum(xhat * gw1, axis=-1, keepdims=True)
        l0 = jnp.mean(a0.reshape(tails, 16, 1), axis=1, keepdims=True) + base0
        l1 = jnp.mean(a1.reshape(tails, 16, 1), axis=1, keepdims=True) + base1
        kind = lax.rem(lax.broadcasted_iota(jnp.int32, (tails, 1, 1), 0), 3)
        sign = jnp.where(kind == 0, -1.0, 1.0)
        g1 = sign / (1.0 + jnp.exp(-sign * (l1 - l0)))
        g1 = jnp.broadcast_to(g1, (tails, 16, 1)).reshape(part, 1)
        moved = (a1 - a0) * (1.0 / (16.0 * width))
        g = (rstd * g1) * ((slope - slope_mean) - xhat * moved)
        gh[r, :] = g
        low_g = g.astype(BF)
        ga[r, :] = low_g
        gc[r, :] = mm(low_g, wo_ref[...], NT).astype(BF)
        both = jnp.where(lax.broadcasted_iota(jnp.int32, (tails, 1, 128), 2) == 0, l0, l1)
        logits_ref[pl.ds(m * tails, tails)] = both
        return 0

    lax.fori_loop(0, rows // part, tail, 0)

    def backward(g, _):
        r = pl.ds(pl.multiple_of(g * unit, 32), unit)
        tr = pl.ds(pl.multiple_of(g * 32, 32), 32)
        for j in range(pairs_of_heads):
            c = slice(j * 128, (j + 1) * 128)
            gcj = gc[r, c]
            gp = mm(gcj, keys_of(g, j, 2 * width), NT)
            p = prob[r, j * 256 : (j + 1) * 256]
            gs, pl_low = [], []
            for h in range(2):
                ph = p[:, h * 128 : (h + 1) * 128]
                gph = gp[:, h * 128 : (h + 1) * 128]
                mean = jnp.sum(gph * ph, axis=-1, keepdims=True)
                gs.append((ph * (gph - mean) * scale).astype(BF))
                pl_low.append(ph.astype(BF))
            gq = mm(jnp.concatenate(gs, axis=1), keys_of(g, j, width), NN)
            gk = mm(jnp.concatenate(gs, axis=0), by_head(qkv[r, c]), TN).astype(BF)
            gv = mm(jnp.concatenate(pl_low, axis=0), by_head(gcj), TN).astype(BF)
            gqkv[r, c] = gq.astype(BF)
            gqkv[r, width + j * 128 : width + (j + 1) * 128] = gk[:96]
            gqkv[r, 2 * width + j * 128 : 2 * width + (j + 1) * 128] = gv[:96]
            gt[tr, c] = gk[96:]
            gt[tr, width + j * 128 : width + (j + 1) * 128] = gv[96:]
        return 0

    lax.fori_loop(0, units, backward, 0)

    def to_rows(m, _):
        r = pl.ds(pl.multiple_of(m * part, 64), part)
        g = mm(gqkv[r, :], w_ref[...], NT) + gh[r, :]
        for k in range(part // 48):
            own = pl.ds(pl.multiple_of(m * (part // 3) + k * 16, 16), 16)
            neg = pl.ds(pl.multiple_of(m * (2 * part // 3) + k * 32, 32), 32)
            own_ref[own, :] = g[k * 48 : k * 48 + 16]
            neg_ref[neg, :] = g[k * 48 + 16 : k * 48 + 48].astype(BF)
        return 0

    lax.fori_loop(0, rows // part, to_rows, 0)
    gtext_ref[...] = mm(gt[...], w_ref[:, width:], NT).astype(BF)

    def weight_step(j, _):
        c = pl.ds(pl.multiple_of(j * col, col), col)
        dw_ref[j] = mm(x_ref[...], gqkv[:, c], TN).astype(BF)
        return 0

    lax.fori_loop(0, width // col, weight_step, 0)

    def weight_text_step(j, _):
        c = pl.ds(pl.multiple_of(j * col + width, col), col)
        ct = pl.ds(pl.multiple_of(j * col, col), col)
        total = mm(x_ref[...], gqkv[:, c], TN) + mm(t_ref[...], gt[:, ct], TN)
        dw_ref[j + width // col] = total.astype(BF)
        return 0

    lax.fori_loop(0, 2 * width // col, weight_text_step, 0)

    def out_step(j, _):
        c = pl.ds(pl.multiple_of(j * col, col), col)
        dw_ref[j + 3 * width // col] = mm(ctx[...], ga[:, c], TN).astype(BF)
        return 0

    lax.fori_loop(0, width // col, out_step, 0)


def attention(images, texts, lens, w, wo, gain, bias, iw, ib):
    rows, width = images.shape
    trows = texts.shape[0]
    vmem = pl.BlockSpec(memory_space=pltpu.VMEM)
    smem = pl.BlockSpec(memory_space=pltpu.SMEM)
    shape = jax.ShapeDtypeStruct
    return pl.pallas_call(
        attention_kernel,
        out_shape=(
            shape((rows // 16, 1, 128), F32),
            shape((trows, width), BF),
            shape((rows // 3, width), F32),
            shape((2 * rows // 3, width), BF),
            shape((4 * width // 256, width, 256), BF),
        ),
        in_specs=[smem, smem] + [vmem] * 7,
        out_specs=(vmem,) * 5,
        scratch_shapes=[
            pltpu.VMEM((rows, 3 * width), BF),
            pltpu.VMEM((trows, 2 * width), BF),
            pltpu.VMEM((rows, width), BF),
            pltpu.VMEM((rows, width), F32),
            pltpu.VMEM((rows, width), BF),
            pltpu.VMEM((rows, width), BF),
            pltpu.VMEM((rows, 3 * width), BF),
            pltpu.VMEM((trows, 2 * width), BF),
            pltpu.VMEM((rows, 2 * width), F32),
        ],
        compiler_params=pltpu.CompilerParams(vmem_limit_bytes=60 * 1024 * 1024),
        name="pair_attention",
    )(lens, ib, images, texts, w, wo, gain.reshape(1, -1), bias.reshape(1, -1), iw.T)


HOLDERS = 48
PIECE = 256
MESH = pl.DeviceIdType.MESH


def place():
    me = lax.axis_index("dp")
    return me, me // 32, (me // 8) % 4, (me // 2) % 4, me % 2


def device_at(z, y, x, core):
    return ((z * 4 + y) * 4 + x) * 2 + core


def holder(piece):
    line, k = piece // 3, piece % 3
    z, y = line // 4, line % 4
    return device_at(z, y, (k + 8 - y - z) % 4, piece % 2)


def held_piece():
    me, z, y, x, core = place()
    k = (x + y + z) % 4
    piece = (z * 4 + y) * 3 + k
    return piece, (k < 3) & (core == piece % 2)


def one_hot(mask):
    return jnp.where(mask, 1.0, 0.0).astype(BF)


def swap_rows(outer, inner):
    n = outer * inner
    to = lax.broadcasted_iota(jnp.int32, (n, n), 0)
    source = lax.broadcasted_iota(jnp.int32, (n, n), 1)
    return one_hot(source == lax.rem(to, outer) * inner + lax.div(to, outer))


def fetch_kernel(q_ref, need_ref, out_ref, table_ref, pieces, held, picked, arrived,
                 send_sem, held_sem, index_send, index_sem, pick_send, pick_sem):
    me = lax.axis_index("dp")
    mine, holding = held_piece()
    peers = held.shape[0]
    slots = arrived.shape[1]
    images = pieces.shape[1]
    swapped = mm(swap_rows(images, 16), q_ref[...], NN).astype(BF)
    for r in range(16):
        for k in range(3):
            pieces[r * 3 + k] = swapped[r * images : (r + 1) * images, k * PIECE : (k + 1) * PIECE]

    def spread(i, _):
        piece = (i + me) % HOLDERS
        target = holder(piece)

        @pl.when(target != me)
        def _():
            pltpu.make_async_remote_copy(
                src_ref=need_ref, dst_ref=table_ref.at[me], send_sem=index_send, recv_sem=index_sem,
                device_id=(target,), device_id_type=MESH).start()
            pltpu.make_async_remote_copy(
                src_ref=pieces.at[piece], dst_ref=held.at[me], send_sem=send_sem, recv_sem=held_sem,
                device_id=(target,), device_id_type=MESH).start()

        @pl.when(target == me)
        def _():
            pltpu.make_async_copy(need_ref, table_ref.at[me], index_sem).start()
            pltpu.make_async_copy(pieces.at[piece], held.at[me], held_sem).start()

        return 0

    lax.fori_loop(0, HOLDERS, spread, 0)

    @pl.when(holding)
    def _():
        pltpu.make_async_copy(table_ref, table_ref, index_sem).wait()
        pltpu.make_async_copy(held, held, held_sem).wait()
        lanes = lax.broadcasted_iota(jnp.int32, (slots, 128), 1)
        lines = lax.broadcasted_iota(jnp.int32, (slots, 128), 0)
        ids = lax.broadcasted_iota(jnp.int32, (1, 2048), 1).astype(F32) + 1.0
        values = held.reshape(2048, PIECE)

        def pick(g, _):
            columns = []
            for b in range(8):
                row = table_ref[g * 8 + b].astype(F32)
                eye = lanes == lines + 32 * (b % 4)
                columns.append(jnp.sum(jnp.where(eye, row, 0.0), axis=-1, keepdims=True))
            hot = one_hot(jnp.concatenate(columns, axis=0) == ids)
            chosen = mm(hot, values[...], NN).astype(BF)
            for b in range(8):
                target = g * 8 + b
                picked[target] = chosen[b * slots : (b + 1) * slots]

                @pl.when(target != me)
                def _():
                    pltpu.make_async_remote_copy(
                        src_ref=picked.at[target], dst_ref=arrived.at[mine], send_sem=pick_send,
                        recv_sem=pick_sem, device_id=(target,), device_id_type=MESH).start()

                @pl.when(target == me)
                def _():
                    pltpu.make_async_copy(picked.at[target], arrived.at[mine], pick_sem).start()

            return 0

        lax.fori_loop(0, peers // 8, pick, 0)

    swap = swap_rows(16, slots)
    pltpu.make_async_copy(arrived, arrived, pick_sem).wait()
    for k in range(3):
        c = slice(k * PIECE, (k + 1) * PIECE)
        stacked = jnp.concatenate([arrived[r * 3 + k] for r in range(16)], axis=0)
        block = mm(swap, stacked, NN).astype(BF)
        for i in range(images):
            out_ref[i * 48 : i * 48 + 16, c] = q_ref[i * 16 : (i + 1) * 16, c]
            out_ref[i * 48 + 16 : i * 48 + 48, c] = block[i * 32 : (i + 1) * 32]

    @pl.when(holding)
    def _():
        pltpu.make_async_copy(pieces.at[0 : HOLDERS - 1], pieces.at[0 : HOLDERS - 1], send_sem).wait()
        pltpu.make_async_copy(table_ref.at[0 : HOLDERS - 1], table_ref.at[0 : HOLDERS - 1], index_send).wait()
        pltpu.make_async_copy(picked.at[0 : peers - 1], picked.at[0 : peers - 1], pick_send).wait()

    @pl.when(jnp.logical_not(holding))
    def _():
        pltpu.make_async_copy(pieces, pieces, send_sem).wait()
        pltpu.make_async_copy(table_ref.at[0:HOLDERS], table_ref.at[0:HOLDERS], index_send).wait()


def fetch(queries, need, peers):
    rows, width = queries.shape
    images = rows // 16
    vmem = pl.BlockSpec(memory_space=pltpu.VMEM)
    return pl.pallas_call(
        fetch_kernel,
        out_shape=(
            jax.ShapeDtypeStruct((3 * rows, width), BF),
            jax.ShapeDtypeStruct((peers, 1, 128), jnp.int32),
        ),
        in_specs=[vmem, vmem],
        out_specs=(vmem, vmem),
        scratch_shapes=[
            pltpu.VMEM((HOLDERS, images, PIECE), BF),
            pltpu.VMEM((peers, images, PIECE), BF),
            pltpu.VMEM((peers, 2 * images, PIECE), BF),
            pltpu.VMEM((HOLDERS, 2 * images, PIECE), BF),
        ]
        + [pltpu.SemaphoreType.DMA] * 6,
        compiler_params=pltpu.CompilerParams(vmem_limit_bytes=48 * 1024 * 1024, has_side_effects=True),
        name="fetch_negatives",
    )(queries, need)


def reduce_kernel(
    g_ref, back_ref, own_ref, table_ref, sum_ref, query_ref,
    half_in, half, in1, sum1, in2, sum2, in3, pieces, held, totals, arrived,
    s_send, s_recv, a_send, a_recv, piece_send, held_sem, total_send, total_sem,
):
    me, z, y, x, core = place()
    mine, holding = held_piece()
    spots = (x, y, z)
    peers, slots = held.shape[0], held.shape[1]
    images = totals.shape[1]
    thirds = range(3)

    def along(axis, step):
        at = [x, y, z]
        at[axis] = (at[axis] + step) % 4
        return device_at(at[2], at[1], at[0], core)

    def axis_of(t, stage):
        return (t + stage) % 3

    twin = me + 1 - 2 * core
    mine_rows = pl.ds(pl.multiple_of(core * 384, 128), 384)
    twin_rows = pl.ds(pl.multiple_of(384 - core * 384, 128), 384)

    def remote(source, target, send, recv, device):
        return pltpu.make_async_remote_copy(
            src_ref=source, dst_ref=target, send_sem=send, recv_sem=recv,
            device_id=(device,), device_id_type=MESH)

    sends = []

    def start(copy):
        copy.start()
        sends.append(copy)

    zero = [
        remote(g_ref.at[pl.ds(4 * t, 4), twin_rows], half_in.at[pl.ds(4 * t, 4)],
               s_send.at[t, 0], s_recv.at[t, 0], twin)
        for t in thirds
    ]
    for copy in zero:
        start(copy)

    swapped = mm(swap_rows(slots, 16), back_ref[...], NN).astype(BF)
    for r in range(16):
        for k in range(3):
            pieces[r * 3 + k] = swapped[r * slots : (r + 1) * slots, k * PIECE : (k + 1) * PIECE]

    def spread(i, _):
        piece = (i + me) % HOLDERS
        target = holder(piece)

        @pl.when(target != me)
        def _():
            remote(pieces.at[piece], held.at[me], piece_send, held_sem, target).start()

        @pl.when(target == me)
        def _():
            pltpu.make_async_copy(pieces.at[piece], held.at[me], held_sem).start()

        return 0

    lax.fori_loop(0, HOLDERS, spread, 0)

    one = {}
    for t in thirds:
        zero[t].wait_recv()
        axis = axis_of(t, 0)

        def add_half(k, _, t=t):
            own = g_ref[4 * t + k, mine_rows, :].astype(F32)
            half[4 * t + k] = (own + half_in[4 * t + k].astype(F32)).astype(BF)
            return 0

        lax.fori_loop(0, 4, add_half, 0)
        for d in (1, 2, 3):
            to = (spots[axis] + d) % 4
            one[t, d] = remote(half.at[4 * t + to], in1.at[t, d - 1],
                               s_send.at[t, d], s_recv.at[t, d], along(axis, d))
            start(one[t, d])

    @pl.when(holding)
    def _():
        pltpu.make_async_copy(held, held, held_sem).wait()
        values = held.reshape(peers * slots, PIECE)
        ids = lax.broadcasted_iota(jnp.int32, (256, 128), 0).astype(F32) + 1.0
        rows = [
            table_ref[4 * b].astype(F32) + table_ref[4 * b + 1].astype(F32)
            + table_ref[4 * b + 2].astype(F32) + table_ref[4 * b + 3].astype(F32)
            for b in range(peers // 4)
        ]

        def add_up(g, _):
            shift = (g * 256).astype(F32)
            hot = jnp.concatenate([one_hot(ids == row - shift) for row in rows], axis=1)
            total = mm(hot, values[...], NN).astype(BF)
            for b in range(16):
                target = g * 16 + b
                totals[target] = total[b * images : (b + 1) * images]

                @pl.when(target != me)
                def _():
                    remote(totals.at[target], arrived.at[mine], total_send, total_sem, target).start()

                @pl.when(target == me)
                def _():
                    pltpu.make_async_copy(totals.at[target], arrived.at[mine], total_sem).start()

            return 0

        lax.fori_loop(0, peers // 16, add_up, 0)

    two = {}
    for t in thirds:
        axis, after = axis_of(t, 0), axis_of(t, 1)
        for d in (1, 2, 3):
            one[t, d].wait_recv()
        total = half[4 * t + spots[axis]].astype(F32)
        for d in range(3):
            total += in1[t, d].astype(F32)
        sum1[t] = total.astype(BF)
        for d in (1, 2, 3):
            to = (spots[after] + d) % 4
            two[t, d] = remote(sum1.at[t, pl.ds(pl.multiple_of(to * 96, 32), 96)], in2.at[t, d - 1],
                               s_send.at[t, 3 + d], s_recv.at[t, 3 + d], along(after, d))
            start(two[t, d])

    def corner(ref, first, spot):
        rows = pl.ds(pl.multiple_of(first + (spot // 2) * 48, 16), 48)
        return ref.at[rows, pl.ds(pl.multiple_of((spot % 2) * 128, 128), 128)]

    three = {}
    for t in thirds:
        axis, after = axis_of(t, 1), axis_of(t, 2)
        for d in (1, 2, 3):
            two[t, d].wait_recv()
        total = sum1[t, pl.ds(pl.multiple_of(spots[axis] * 96, 32), 96), :].astype(F32)
        for d in range(3):
            total += in2[t, d].astype(F32)
        sum2[t] = total.astype(BF)
        for d in (1, 2, 3):
            to = (spots[after] + d) % 4
            three[t, d] = remote(corner(sum2.at[t], 0, to), in3.at[t, d - 1],
                                 s_send.at[t, 6 + d], s_recv.at[t, 6 + d], along(after, d))
            start(three[t, d])

    last = {}
    for t in thirds:
        axis = axis_of(t, 2)
        for d in (1, 2, 3):
            three[t, d].wait_recv()
        total = corner(sum2.at[t], 0, spots[axis])[...].astype(F32)
        for d in range(3):
            total += in3[t, d].astype(F32)
        block = sum_ref.at[4 * t + spots[axis_of(t, 0)]]
        first = core * 384 + spots[axis_of(t, 1)] * 96
        piece = corner(block, first, spots[axis])
        piece[...] = total.astype(BF)
        for d in (1, 2, 3):
            last[t, d] = remote(piece, piece, a_send.at[t, d], a_recv.at[t, d], along(axis, d))
            start(last[t, d])

    def came(t, stage, ref, d):
        return pltpu.make_async_copy(ref, ref, a_recv.at[t, stage * 3 + d])

    for t in thirds:
        axis = axis_of(t, 1)
        block = sum_ref.at[4 * t + spots[axis_of(t, 0)]]
        first = core * 384 + spots[axis] * 96
        for d in (1, 2, 3):
            came(t, 0, corner(block, first, (spots[axis_of(t, 2)] + 4 - d) % 4), d).wait()
        piece = block.at[pl.ds(pl.multiple_of(first, 32), 96)]
        for d in (1, 2, 3):
            start(remote(piece, piece, a_send.at[t, 3 + d], a_recv.at[t, 3 + d], along(axis, d)))

    for t in thirds:
        axis = axis_of(t, 0)
        block = sum_ref.at[4 * t + spots[axis]]
        for d in (1, 2, 3):
            spot = (spots[axis_of(t, 1)] + 4 - d) % 4
            came(t, 1, block.at[pl.ds(pl.multiple_of(core * 384 + spot * 96, 32), 96)], d).wait()
        piece = block.at[mine_rows]
        for d in (1, 2, 3):
            start(remote(piece, piece, a_send.at[t, 6 + d], a_recv.at[t, 6 + d], along(axis, d)))

    for t in thirds:
        axis = axis_of(t, 0)
        for d in (1, 2, 3):
            spot = (spots[axis] + 4 - d) % 4
            came(t, 2, sum_ref.at[4 * t + spot, mine_rows], d).wait()
        piece = sum_ref.at[pl.ds(4 * t, 4), mine_rows]
        start(remote(piece, piece, a_send.at[t, 0], a_recv.at[t, 0], twin))

    pltpu.make_async_copy(arrived, arrived, total_sem).wait()
    swap = swap_rows(16, images)
    for k in range(3):
        c = slice(k * PIECE, (k + 1) * PIECE)
        stacked = jnp.concatenate([arrived[r * 3 + k] for r in range(16)], axis=0)
        query_ref[:, c] = (own_ref[:, c] + mm(swap, stacked, NN)).astype(BF)

    for t in thirds:
        other = sum_ref.at[pl.ds(4 * t, 4), twin_rows]
        pltpu.make_async_copy(other, other, a_recv.at[t, 0]).wait()
    for copy in sends:
        copy.wait_send()

    @pl.when(holding)
    def _():
        pltpu.make_async_copy(pieces.at[0 : HOLDERS - 1], pieces.at[0 : HOLDERS - 1], piece_send).wait()
        pltpu.make_async_copy(totals.at[0 : peers - 1], totals.at[0 : peers - 1], total_send).wait()

    @pl.when(jnp.logical_not(holding))
    def _():
        pltpu.make_async_copy(pieces, pieces, piece_send).wait()


def reduce(grads, back, own, table):
    peers = table.shape[0]
    rows, width = own.shape
    images = rows // 16
    vmem = pl.BlockSpec(memory_space=pltpu.VMEM)
    dma = pltpu.SemaphoreType.DMA
    return pl.pallas_call(
        reduce_kernel,
        out_shape=(
            jax.ShapeDtypeStruct(grads.shape, BF),
            jax.ShapeDtypeStruct(own.shape, BF),
        ),
        in_specs=[vmem] * 4,
        out_specs=(vmem, vmem),
        scratch_shapes=[
            pltpu.VMEM((12, 384, 256), BF),
            pltpu.VMEM((12, 384, 256), BF),
            pltpu.VMEM((3, 3, 384, 256), BF),
            pltpu.VMEM((3, 384, 256), BF),
            pltpu.VMEM((3, 3, 96, 256), BF),
            pltpu.VMEM((3, 96, 256), BF),
            pltpu.VMEM((3, 3, 48, 128), BF),
            pltpu.VMEM((HOLDERS, 2 * images, PIECE), BF),
            pltpu.VMEM((peers, 2 * images, PIECE), BF),
            pltpu.VMEM((peers, images, PIECE), BF),
            pltpu.VMEM((HOLDERS, images, PIECE), BF),
            dma((3, 10)), dma((3, 10)), dma((3, 10)), dma((3, 10)),
            dma, dma, dma, dma,
        ],
        compiler_params=pltpu.CompilerParams(vmem_limit_bytes=56 * 1024 * 1024, has_side_effects=True),
        name="sum_gradients",
    )(grads, back, own, table)


def on_device(
    text_states, text_len, query_states, neg_owner, neg_slot,
    projection_weight, output_weight, ln_gain, ln_bias, itm_weight, itm_bias,
):
    captions, query_rows, width = query_states.shape
    peers = lax.axis_size("dp")
    me = lax.axis_index("dp")
    wanted = (captions * neg_owner + neg_slot + 1).reshape(1, 2 * captions)
    group = jnp.arange(4)[:, None] == me % 4
    need = jnp.where(group, wanted, 0).reshape(1, 128)
    images, table = fetch(query_states.reshape(-1, width), need, peers)
    logits, grad_text, own, back, grads = attention(
        images, text_states.reshape(-1, width), text_len,
        projection_weight, output_weight, ln_gain, ln_bias, itm_weight, itm_bias,
    )
    sums, grad_query = reduce(grads, back, own, table)
    share = 1.0 / (captions * peers)
    sums = sums.transpose(1, 0, 2).reshape(width, 4 * width).astype(F32) * share
    return (
        logits[:, 0, :2].reshape(captions, 3, 2),
        grad_text.reshape(text_states.shape),
        grad_query.reshape(query_states.shape),
        sums[:, : 3 * width],
        sums[:, 3 * width :],
    )


def solution(mesh):
    rows = P("dp", None, None)
    placed = (rows, P("dp"), rows, P("dp", None), P("dp", None)) + (P(),) * 6
    return jax.shard_map(
        on_device, mesh=mesh, in_specs=placed, out_specs=(rows, rows, rows, P(), P()), check_vma=False
    )
```

```python
import math
import jax
import jax.numpy as jnp
from jax import lax
from jax.experimental import pallas as pl
from jax.experimental.pallas import tpu as pltpu
from jax.sharding import PartitionSpec as P

F32 = jnp.float32
BF = jnp.bfloat16
NN = (((1,), (0,)), ((), ()))
NT = (((1,), (1,)), ((), ()))
TN = (((0,), (0,)), ((), ()))


def mm(a, b, dims):
    return lax.dot_general(a, b, dims, preferred_element_type=F32)


HOLDERS = 48
PIECE = 256
MESH = pl.DeviceIdType.MESH


def place():
    me = lax.axis_index("dp")
    return me, me // 32, (me // 8) % 4, (me // 2) % 4, me % 2


def device_at(z, y, x, core):
    return ((z * 4 + y) * 4 + x) * 2 + core


def holder(piece):
    line, k = piece // 3, piece % 3
    z, y = line // 4, line % 4
    return device_at(z, y, (k + 8 - y - z) % 4, piece % 2)


def held_piece():
    me, z, y, x, core = place()
    k = (x + y + z) % 4
    piece = (z * 4 + y) * 3 + k
    return piece, (k < 3) & (core == piece % 2)


def one_hot(mask):
    return jnp.where(mask, 1.0, 0.0).astype(BF)


def swap_rows(outer, inner):
    n = outer * inner
    to = lax.broadcasted_iota(jnp.int32, (n, n), 0)
    source = lax.broadcasted_iota(jnp.int32, (n, n), 1)
    return one_hot(source == lax.rem(to, outer) * inner + lax.div(to, outer))


def pair_kernel(
    lens, ibias, need_ref, q_ref, t_ref, w_ref, wo_ref, gain_ref, bias_ref, iw_ref,
    logits_ref, gtext_ref, query_ref, sum_ref,
    x, qkv, tkv, ctx, gh, ga, gc, gqkv, gt, prob, own_grad, back, grads,
    table, pieces, held, picked, arrived, back_pieces, back_held, totals, back_arrived,
    half_in, in1, sum1, in2, sum2, in3,
    ready, index_send, index_sem, piece_send, held_sem, pick_send, pick_sem,
    back_send, back_sem, total_send, total_sem,
    half_send, half_recv, s_send, s_recv, a_send, a_recv, twin_send, twin_recv,
):
    rows, width = x.shape
    me, z, y, pos_x, core = place()
    mine, holding = held_piece()
    spots = (pos_x, y, z)
    peers, images = held.shape[0], held.shape[1]
    slots = arrived.shape[1]
    pairs_of_heads = width // 128
    unit = 96
    units = rows // unit
    scale = 1.0 / math.sqrt(64.0)
    col = 256
    thirds = range(3)

    def along(axis, step):
        at = [pos_x, y, z]
        at[axis] = (at[axis] + step) % 4
        return device_at(at[2], at[1], at[0], core)

    def axis_of(t, stage):
        return (t + stage) % 3

    twin = me + 1 - 2 * core
    mine_rows = pl.ds(pl.multiple_of(core * 384, 128), 384)
    twin_rows = pl.ds(pl.multiple_of(384 - core * 384, 128), 384)

    def remote(source, target, send, recv, device):
        return pltpu.make_async_remote_copy(
            src_ref=source, dst_ref=target, send_sem=send, recv_sem=recv,
            device_id=(device,), device_id_type=MESH)

    def greet(semaphore, axis):
        for d in (1, 2, 3):
            pl.semaphore_signal(semaphore, inc=1, device_id=(along(axis, d),), device_id_type=MESH)

    barrier = pltpu.get_barrier_semaphore()
    for axis in range(3):
        greet(barrier, axis)
    pl.semaphore_signal(barrier, inc=1, device_id=(twin,), device_id_type=MESH)
    pl.semaphore_wait(barrier, 10)

    pl.semaphore_signal(ready.at[3], inc=1, device_id=(twin,), device_id_type=MESH)
    swapped = mm(swap_rows(images, 16), q_ref[...], NN).astype(BF)
    for r in range(16):
        for k in range(3):
            pieces[r * 3 + k] = swapped[r * images : (r + 1) * images, k * PIECE : (k + 1) * PIECE]
    pl.semaphore_wait(ready.at[3], 1)
    greet(ready.at[0], 0)

    def tkv_step(j, _):
        c = pl.ds(pl.multiple_of(j * col, col), col)
        cw = pl.ds(pl.multiple_of(j * col + width, col), col)
        tkv[:, c] = mm(t_ref[...], w_ref[:, cw], NN).astype(BF)
        return 0

    lax.fori_loop(0, 2, tkv_step, 0)
    pl.semaphore_wait(ready.at[0], 3)
    greet(ready.at[1], 1)
    lax.fori_loop(2, 4, tkv_step, 0)
    pl.semaphore_wait(ready.at[1], 3)
    greet(ready.at[2], 2)
    lax.fori_loop(4, 6, tkv_step, 0)
    pl.semaphore_wait(ready.at[2], 3)

    def spread(i, _):
        piece = (i + me) % HOLDERS
        target = holder(piece)

        @pl.when(target != me)
        def _():
            remote(need_ref, table.at[me], index_send, index_sem, target).start()
            remote(pieces.at[piece], held.at[me], piece_send, held_sem, target).start()

        @pl.when(target == me)
        def _():
            pltpu.make_async_copy(need_ref, table.at[me], index_sem).start()
            pltpu.make_async_copy(pieces.at[piece], held.at[me], held_sem).start()

        return 0

    lax.fori_loop(0, HOLDERS, spread, 0)

    def own_step(j, _):
        c = pl.ds(pl.multiple_of(j * col, col), col)
        got = mm(q_ref[...], w_ref[:, c], NN).astype(BF)
        for i in range(images):
            qkv[i * 48 : i * 48 + 16, c] = got[i * 16 : (i + 1) * 16]
        return 0

    lax.fori_loop(0, 3 * width // col, own_step, 0)

    @pl.when(holding)
    def _():
        pltpu.make_async_copy(table, table, index_sem).wait()
        pltpu.make_async_copy(held, held, held_sem).wait()
        lanes = lax.broadcasted_iota(jnp.int32, (slots, 128), 1)
        lines = lax.broadcasted_iota(jnp.int32, (slots, 128), 0)
        ids = lax.broadcasted_iota(jnp.int32, (1, 2048), 1).astype(F32) + 1.0
        values = held.reshape(2048, PIECE)

        def pick(g, _):
            columns = []
            for b in range(8):
                row = table[g * 8 + b].astype(F32)
                eye = lanes == lines + 32 * (b % 4)
                columns.append(jnp.sum(jnp.where(eye, row, 0.0), axis=-1, keepdims=True))
            hot = one_hot(jnp.concatenate(columns, axis=0) == ids)
            chosen = mm(hot, values[...], NN).astype(BF)
            for b in range(8):
                target = g * 8 + b
                picked[target] = chosen[b * slots : (b + 1) * slots]

                @pl.when(target != me)
                def _():
                    remote(picked.at[target], arrived.at[mine], pick_send, pick_sem, target).start()

                @pl.when(target == me)
                def _():
                    pltpu.make_async_copy(picked.at[target], arrived.at[mine], pick_sem).start()

            return 0

        lax.fori_loop(0, peers // 8, pick, 0)

    swap = swap_rows(16, slots)
    pltpu.make_async_copy(arrived, arrived, pick_sem).wait()
    for k in range(3):
        c = slice(k * PIECE, (k + 1) * PIECE)
        stacked = jnp.concatenate([arrived[r * 3 + k] for r in range(16)], axis=0)
        block = mm(swap, stacked, NN).astype(BF)
        for i in range(images):
            x[i * 48 : i * 48 + 16, c] = q_ref[i * 16 : (i + 1) * 16, c]
            x[i * 48 + 16 : i * 48 + 48, c] = block[i * 32 : (i + 1) * 32]
            back[i * 32 : (i + 1) * 32, c] = block[i * 32 : (i + 1) * 32]

    def negative_step(j, _):
        c = pl.ds(pl.multiple_of(j * col, col), col)
        got = mm(back[...], w_ref[:, c], NN).astype(BF)
        for i in range(images):
            qkv[i * 48 + 16 : i * 48 + 48, c] = got[i * 32 : (i + 1) * 32]
        return 0

    lax.fori_loop(0, 3 * width // col, negative_step, 0)

    lane = lax.broadcasted_iota(jnp.int32, (1, 128), 1)
    low = lane < 64

    def by_head(a):
        zero = jnp.zeros_like(a)
        return jnp.concatenate([jnp.where(low, a, zero), jnp.where(low, zero, a)], axis=0)

    def keys_of(g, j, first):
        r = pl.ds(pl.multiple_of(g * unit, 32), unit)
        tr = pl.ds(pl.multiple_of(g * 32, 32), 32)
        image = qkv[r, first + j * 128 : first + (j + 1) * 128]
        text = tkv[tr, first - width + j * 128 : first - width + (j + 1) * 128]
        return by_head(jnp.concatenate([image, text], axis=0))

    def forward(g, _):
        r = pl.ds(pl.multiple_of(g * unit, 32), unit)
        rowi = lax.broadcasted_iota(jnp.int32, (unit, 128), 0)
        lanei = lax.broadcasted_iota(jnp.int32, (unit, 128), 1)
        first = rowi < 48
        start = jnp.where(first, 96, 112)
        live = jnp.where(first, lens[2 * g], lens[2 * g + 1])
        block = rowi - lax.rem(rowi, 16)
        valid = ((lanei >= block) & (lanei < block + 16)) | ((lanei >= start) & (lanei < start + live))
        for j in range(pairs_of_heads):
            q = qkv[r, j * 128 : (j + 1) * 128]
            s = mm(q, keys_of(g, j, width), NT) * scale
            parts = []
            for h in range(2):
                sh = jnp.where(valid, s[:, h * 128 : (h + 1) * 128], -1e30)
                e = jnp.exp(sh - jnp.max(sh, axis=-1, keepdims=True))
                parts.append(e * (1.0 / jnp.sum(e, axis=-1, keepdims=True)))
            p = jnp.concatenate(parts, axis=1)
            prob[r, j * 256 : (j + 1) * 256] = p
            ctx[r, j * 128 : (j + 1) * 128] = mm(p.astype(BF), keys_of(g, j, 2 * width), NN).astype(BF)
        return 0

    lax.fori_loop(0, units, forward, 0)

    gw0 = gain_ref[...].reshape(1, -1) * iw_ref[0:1, :]
    gw1 = gain_ref[...].reshape(1, -1) * iw_ref[1:2, :]
    slope = (gw1 - gw0) * (1.0 / 16.0)
    slope_mean = jnp.mean(slope)
    base0 = jnp.sum(bias_ref[...].reshape(1, -1) * iw_ref[0:1, :]) + ibias[0]
    base1 = jnp.sum(bias_ref[...].reshape(1, -1) * iw_ref[1:2, :]) + ibias[1]
    part = 192
    tails = part // 16

    def tail(m, _):
        r = pl.ds(pl.multiple_of(m * part, 64), part)
        h = x[r, :].astype(F32) + mm(ctx[r, :], wo_ref[...], NN)
        center = h - jnp.mean(h, axis=-1, keepdims=True)
        spread = jnp.mean(center * center, axis=-1, keepdims=True)
        rstd = lax.rsqrt(spread + 1e-6)
        xhat = center * rstd
        a0 = jnp.sum(xhat * gw0, axis=-1, keepdims=True)
        a1 = jnp.sum(xhat * gw1, axis=-1, keepdims=True)
        l0 = jnp.mean(a0.reshape(tails, 16, 1), axis=1, keepdims=True) + base0
        l1 = jnp.mean(a1.reshape(tails, 16, 1), axis=1, keepdims=True) + base1
        kind = lax.rem(lax.broadcasted_iota(jnp.int32, (tails, 1, 1), 0), 3)
        sign = jnp.where(kind == 0, -1.0, 1.0)
        g1 = sign / (1.0 + jnp.exp(-sign * (l1 - l0)))
        g1 = jnp.broadcast_to(g1, (tails, 16, 1)).reshape(part, 1)
        moved = (a1 - a0) * (1.0 / (16.0 * width))
        g = (rstd * g1) * ((slope - slope_mean) - xhat * moved)
        gh[r, :] = g
        low_g = g.astype(BF)
        ga[r, :] = low_g
        gc[r, :] = mm(low_g, wo_ref[...], NT).astype(BF)
        both = jnp.where(lax.broadcasted_iota(jnp.int32, (tails, 1, 128), 2) == 0, l0, l1)
        logits_ref[pl.ds(m * tails, tails)] = both
        return 0

    lax.fori_loop(0, rows // part, tail, 0)

    def backward(g, _):
        r = pl.ds(pl.multiple_of(g * unit, 32), unit)
        tr = pl.ds(pl.multiple_of(g * 32, 32), 32)
        for j in range(pairs_of_heads):
            c = slice(j * 128, (j + 1) * 128)
            gcj = gc[r, c]
            gp = mm(gcj, keys_of(g, j, 2 * width), NT)
            p = prob[r, j * 256 : (j + 1) * 256]
            gs, pl_low = [], []
            for h in range(2):
                ph = p[:, h * 128 : (h + 1) * 128]
                gph = gp[:, h * 128 : (h + 1) * 128]
                mean = jnp.sum(gph * ph, axis=-1, keepdims=True)
                gs.append((ph * (gph - mean) * scale).astype(BF))
                pl_low.append(ph.astype(BF))
            gq = mm(jnp.concatenate(gs, axis=1), keys_of(g, j, width), NN)
            gk = mm(jnp.concatenate(gs, axis=0), by_head(qkv[r, c]), TN).astype(BF)
            gv = mm(jnp.concatenate(pl_low, axis=0), by_head(gcj), TN).astype(BF)
            gqkv[r, c] = gq.astype(BF)
            gqkv[r, width + j * 128 : width + (j + 1) * 128] = gk[:96]
            gqkv[r, 2 * width + j * 128 : 2 * width + (j + 1) * 128] = gv[:96]
            gt[tr, c] = gk[96:]
            gt[tr, width + j * 128 : width + (j + 1) * 128] = gv[96:]
        return 0

    lax.fori_loop(0, units, backward, 0)

    def to_rows(m, _):
        r = pl.ds(pl.multiple_of(m * part, 64), part)
        g = mm(gqkv[r, :], w_ref[...], NT) + gh[r, :]
        for k in range(part // 48):
            own = pl.ds(pl.multiple_of(m * (part // 3) + k * 16, 16), 16)
            neg = pl.ds(pl.multiple_of(m * (2 * part // 3) + k * 32, 32), 32)
            own_grad[own, :] = g[k * 48 : k * 48 + 16]
            back[neg, :] = g[k * 48 + 16 : k * 48 + 48].astype(BF)
        return 0

    lax.fori_loop(0, rows // part, to_rows, 0)


    swapped = mm(swap_rows(slots, 16), back[...], NN).astype(BF)
    for r in range(16):
        for k in range(3):
            back_pieces[r * 3 + k] = swapped[r * slots : (r + 1) * slots, k * PIECE : (k + 1) * PIECE]

    def spread_back(i, _):
        piece = (i + me) % HOLDERS
        target = holder(piece)

        @pl.when(target != me)
        def _():
            remote(back_pieces.at[piece], back_held.at[me], back_send, back_sem, target).start()

        @pl.when(target == me)
        def _():
            pltpu.make_async_copy(back_pieces.at[piece], back_held.at[me], back_sem).start()

        return 0

    lax.fori_loop(0, HOLDERS, spread_back, 0)

    def half_copy(j):
        return remote(grads.at[j, twin_rows], half_in.at[j], half_send.at[j], half_recv.at[j], twin)

    def weight_step(j, _):
        c = pl.ds(pl.multiple_of(j * col, col), col)
        grads[j] = mm(x[...], gqkv[:, c], TN).astype(BF)
        half_copy(j).start()
        return 0

    lax.fori_loop(0, width // col, weight_step, 0)

    def weight_text_step(j, _):
        c = pl.ds(pl.multiple_of(j * col, col), col)
        ct = pl.ds(pl.multiple_of(j * col - width, col), col)
        grads[j] = (mm(x[...], gqkv[:, c], TN) + mm(t_ref[...], gt[:, ct], TN)).astype(BF)
        half_copy(j).start()
        return 0

    lax.fori_loop(width // col, 3 * width // col, weight_text_step, 0)

    def out_step(j, _):
        c = pl.ds(pl.multiple_of(j * col - 3 * width, col), col)
        grads[j] = mm(ctx[...], ga[:, c], TN).astype(BF)
        half_copy(j).start()
        return 0

    lax.fori_loop(3 * width // col, 4 * width // col, out_step, 0)

    sends = []

    def start(copy):
        copy.start()
        sends.append(copy)

    one = {}
    for t in thirds:
        axis = axis_of(t, 0)

        def add_half(k, _, t=t):
            half_copy(4 * t + k).wait_recv()
            own = grads[4 * t + k, mine_rows, :].astype(F32)
            half_in[4 * t + k] = (own + half_in[4 * t + k].astype(F32)).astype(BF)
            return 0

        lax.fori_loop(0, 4, add_half, 0)
        for d in (1, 2, 3):
            to = (spots[axis] + d) % 4
            one[t, d] = remote(half_in.at[4 * t + to], in1.at[t, d - 1],
                               s_send.at[t, d], s_recv.at[t, d], along(axis, d))
            start(one[t, d])

    @pl.when(holding)
    def _():
        pltpu.make_async_copy(back_held, back_held, back_sem).wait()
        values = back_held.reshape(peers * slots, PIECE)
        ids = lax.broadcasted_iota(jnp.int32, (256, 128), 0).astype(F32) + 1.0
        rows = [
            table[4 * b].astype(F32) + table[4 * b + 1].astype(F32)
            + table[4 * b + 2].astype(F32) + table[4 * b + 3].astype(F32)
            for b in range(peers // 4)
        ]

        def add_up(g, _):
            shift = (g * 256).astype(F32)
            hot = jnp.concatenate([one_hot(ids == row - shift) for row in rows], axis=1)
            total = mm(hot, values[...], NN).astype(BF)
            for b in range(16):
                target = g * 16 + b
                totals[target] = total[b * images : (b + 1) * images]

                @pl.when(target != me)
                def _():
                    remote(totals.at[target], back_arrived.at[mine], total_send, total_sem, target).start()

                @pl.when(target == me)
                def _():
                    pltpu.make_async_copy(totals.at[target], back_arrived.at[mine], total_sem).start()

            return 0

        lax.fori_loop(0, peers // 16, add_up, 0)


    gtext_ref[...] = mm(gt[...], w_ref[:, width:], NT).astype(BF)

    two = {}
    for t in thirds:
        axis, after = axis_of(t, 0), axis_of(t, 1)
        for d in (1, 2, 3):
            one[t, d].wait_recv()
        total = half_in[4 * t + spots[axis]].astype(F32)
        for d in range(3):
            total += in1[t, d].astype(F32)
        sum1[t] = total.astype(BF)
        for d in (1, 2, 3):
            to = (spots[after] + d) % 4
            two[t, d] = remote(sum1.at[t, pl.ds(pl.multiple_of(to * 96, 32), 96)], in2.at[t, d - 1],
                               s_send.at[t, 3 + d], s_recv.at[t, 3 + d], along(after, d))
            start(two[t, d])

    def corner(ref, first, spot):
        rows = pl.ds(pl.multiple_of(first + (spot // 2) * 48, 16), 48)
        return ref.at[rows, pl.ds(pl.multiple_of((spot % 2) * 128, 128), 128)]

    three = {}
    for t in thirds:
        axis, after = axis_of(t, 1), axis_of(t, 2)
        for d in (1, 2, 3):
            two[t, d].wait_recv()
        total = sum1[t, pl.ds(pl.multiple_of(spots[axis] * 96, 32), 96), :].astype(F32)
        for d in range(3):
            total += in2[t, d].astype(F32)
        sum2[t] = total.astype(BF)
        for d in (1, 2, 3):
            to = (spots[after] + d) % 4
            three[t, d] = remote(corner(sum2.at[t], 0, to), in3.at[t, d - 1],
                                 s_send.at[t, 6 + d], s_recv.at[t, 6 + d], along(after, d))
            start(three[t, d])

    last = {}
    for t in thirds:
        axis = axis_of(t, 2)
        for d in (1, 2, 3):
            three[t, d].wait_recv()
        total = corner(sum2.at[t], 0, spots[axis])[...].astype(F32)
        for d in range(3):
            total += in3[t, d].astype(F32)
        block = sum_ref.at[4 * t + spots[axis_of(t, 0)]]
        first = core * 384 + spots[axis_of(t, 1)] * 96
        piece = corner(block, first, spots[axis])
        piece[...] = total.astype(BF)
        for d in (1, 2, 3):
            last[t, d] = remote(piece, piece, a_send.at[t, d], a_recv.at[t, d], along(axis, d))
            start(last[t, d])

    def came(t, stage, ref, d):
        return pltpu.make_async_copy(ref, ref, a_recv.at[t, stage * 3 + d])

    for t in thirds:
        axis = axis_of(t, 1)
        block = sum_ref.at[4 * t + spots[axis_of(t, 0)]]
        first = core * 384 + spots[axis] * 96
        for d in (1, 2, 3):
            came(t, 0, corner(block, first, (spots[axis_of(t, 2)] + 4 - d) % 4), d).wait()
        piece = block.at[pl.ds(pl.multiple_of(first, 32), 96)]
        for d in (1, 2, 3):
            start(remote(piece, piece, a_send.at[t, 3 + d], a_recv.at[t, 3 + d], along(axis, d)))

    for t in thirds:
        axis = axis_of(t, 0)
        block = sum_ref.at[4 * t + spots[axis]]
        for d in (1, 2, 3):
            spot = (spots[axis_of(t, 1)] + 4 - d) % 4
            came(t, 1, block.at[pl.ds(pl.multiple_of(core * 384 + spot * 96, 32), 96)], d).wait()
        piece = block.at[mine_rows]
        start(remote(piece, piece, twin_send.at[t, 0], twin_recv.at[t, 0], twin))
        for d in (1, 2, 3):
            start(remote(piece, piece, a_send.at[t, 6 + d], a_recv.at[t, 6 + d], along(axis, d)))

    for t in thirds:
        axis = axis_of(t, 0)
        for d in (1, 2, 3):
            piece = sum_ref.at[4 * t + (spots[axis] + 4 - d) % 4, mine_rows]
            came(t, 2, piece, d).wait()
            start(remote(piece, piece, twin_send.at[t, d], twin_recv.at[t, d], twin))


    pltpu.make_async_copy(back_arrived, back_arrived, total_sem).wait()
    swap = swap_rows(16, images)
    for k in range(3):
        c = slice(k * PIECE, (k + 1) * PIECE)
        stacked = jnp.concatenate([back_arrived[r * 3 + k] for r in range(16)], axis=0)
        query_ref[:, c] = (own_grad[:, c] + mm(swap, stacked, NN)).astype(BF)

    for t in thirds:
        for d in range(4):
            other = sum_ref.at[4 * t + (spots[axis_of(t, 0)] + 4 - d) % 4, twin_rows]
            pltpu.make_async_copy(other, other, twin_recv.at[t, d]).wait()
    for copy in sends:
        copy.wait_send()

    def half_sent(j, _):
        half_copy(j).wait_send()
        return 0

    lax.fori_loop(0, 4 * width // col, half_sent, 0)

    def sent(ref, count, semaphore):
        pltpu.make_async_copy(ref.at[0:count], ref.at[0:count], semaphore).wait()

    @pl.when(holding)
    def _():
        sent(pieces, HOLDERS - 1, piece_send)
        sent(table, HOLDERS - 1, index_send)
        sent(picked, peers - 1, pick_send)
        sent(back_pieces, HOLDERS - 1, back_send)
        sent(totals, peers - 1, total_send)

    @pl.when(jnp.logical_not(holding))
    def _():
        sent(pieces, HOLDERS, piece_send)
        sent(table, HOLDERS, index_send)
        sent(back_pieces, HOLDERS, back_send)


def pair_losses(lens, ib, need, queries, texts, w, wo, gain, bias, iw, peers):
    own, width = queries.shape
    rows, trows = 3 * own, texts.shape[0]
    images = own // 16
    vmem = pl.BlockSpec(memory_space=pltpu.VMEM)
    smem = pl.BlockSpec(memory_space=pltpu.SMEM)
    shape = jax.ShapeDtypeStruct
    dma = pltpu.SemaphoreType.DMA
    return pl.pallas_call(
        pair_kernel,
        out_shape=(
            shape((rows // 16, 1, 128), F32),
            shape((trows, width), BF),
            shape((own, width), BF),
            shape((12, width, 256), BF),
        ),
        in_specs=[smem, smem] + [vmem] * 8,
        out_specs=(vmem,) * 4,
        scratch_shapes=[
            pltpu.VMEM((rows, width), BF),
            pltpu.VMEM((rows, 3 * width), BF),
            pltpu.VMEM((trows, 2 * width), BF),
            pltpu.VMEM((rows, width), BF),
            pltpu.VMEM((rows, width), F32),
            pltpu.VMEM((rows, width), BF),
            pltpu.VMEM((rows, width), BF),
            pltpu.VMEM((rows, 3 * width), BF),
            pltpu.VMEM((trows, 2 * width), BF),
            pltpu.VMEM((rows, 2 * width), F32),
            pltpu.VMEM((own, width), F32),
            pltpu.VMEM((2 * own, width), BF),
            pltpu.VMEM((12, width, 256), BF),
            pltpu.VMEM((peers, 1, 128), jnp.int32),
            pltpu.VMEM((HOLDERS, images, PIECE), BF),
            pltpu.VMEM((peers, images, PIECE), BF),
            pltpu.VMEM((peers, 2 * images, PIECE), BF),
            pltpu.VMEM((HOLDERS, 2 * images, PIECE), BF),
            pltpu.VMEM((HOLDERS, 2 * images, PIECE), BF),
            pltpu.VMEM((peers, 2 * images, PIECE), BF),
            pltpu.VMEM((peers, images, PIECE), BF),
            pltpu.VMEM((HOLDERS, images, PIECE), BF),
            pltpu.VMEM((12, 384, 256), BF),
            pltpu.VMEM((3, 3, 384, 256), BF),
            pltpu.VMEM((3, 384, 256), BF),
            pltpu.VMEM((3, 3, 96, 256), BF),
            pltpu.VMEM((3, 96, 256), BF),
            pltpu.VMEM((3, 3, 48, 128), BF),
            pltpu.SemaphoreType.REGULAR((4,)),
            dma, dma, dma, dma, dma, dma, dma, dma, dma, dma,
            dma((12,)), dma((12,)), dma((3, 10)), dma((3, 10)), dma((3, 10)), dma((3, 10)),
            dma((3, 4)), dma((3, 4)),
        ],
        compiler_params=pltpu.CompilerParams(
            vmem_limit_bytes=63 * 1024 * 1024, has_side_effects=True, collective_id=0
        ),
        name="pair_losses",
    )(lens, ib, need, queries, texts, w, wo, gain, bias, iw.T)


def widen_kernel(share, sum_ref, qkv_ref, out_ref):
    j = pl.program_id(0)

    @pl.when(j < 9)
    def _():
        qkv_ref[...] = sum_ref[0].astype(F32) * share

    @pl.when(j >= 9)
    def _():
        out_ref[...] = sum_ref[0].astype(F32) * share


def widen(sums, share):
    width = sums.shape[1]
    return pl.pallas_call(
        lambda *refs: widen_kernel(share, *refs),
        grid=(12,),
        out_shape=(
            jax.ShapeDtypeStruct((width, 3 * width), F32),
            jax.ShapeDtypeStruct((width, width), F32),
        ),
        in_specs=[pl.BlockSpec((1, width, 256), lambda j: (j, 0, 0))],
        out_specs=(
            pl.BlockSpec((width, 256), lambda j: (0, jnp.minimum(j, 8))),
            pl.BlockSpec((width, 256), lambda j: (0, jnp.maximum(j - 9, 0))),
        ),
        name="widen",
    )(sums)


def on_device(
    text_states, text_len, query_states, neg_owner, neg_slot,
    projection_weight, output_weight, ln_gain, ln_bias, itm_weight, itm_bias,
):
    captions, query_rows, width = query_states.shape
    peers = lax.axis_size("dp")
    me = lax.axis_index("dp")
    wanted = (captions * neg_owner + neg_slot + 1).reshape(1, 2 * captions)
    group = jnp.arange(4)[:, None] == me % 4
    need = jnp.where(group, wanted, 0).reshape(1, 128)
    logits, grad_text, grad_query, sums = pair_losses(
        text_len, itm_bias, need, query_states.reshape(-1, width), text_states.reshape(-1, width),
        projection_weight, output_weight, ln_gain, ln_bias, itm_weight, peers,
    )
    sum_qkv, sum_out = widen(sums, 1.0 / (captions * peers))
    return (
        logits[:, 0, :2].reshape(captions, 3, 2),
        grad_text.reshape(text_states.shape),
        grad_query.reshape(query_states.shape),
        sum_qkv,
        sum_out,
    )


def solution(mesh):
    rows = P("dp", None, None)
    placed = (rows, P("dp"), rows, P("dp", None), P("dp", None)) + (P(),) * 6
    return jax.shard_map(
        on_device, mesh=mesh, in_specs=placed, out_specs=(rows, rows, rows, P(), P()), check_vma=False
    )
```

```python
import math
import jax
import jax.numpy as jnp
from jax import lax
from jax.experimental import pallas as pl
from jax.experimental.pallas import tpu as pltpu
from jax.sharding import PartitionSpec as P

F32 = jnp.float32
BF = jnp.bfloat16
NN = (((1,), (0,)), ((), ()))
NT = (((1,), (1,)), ((), ()))
TN = (((0,), (0,)), ((), ()))


def mm(a, b, dims):
    return lax.dot_general(a, b, dims, preferred_element_type=F32)


HOLDERS = 48
PIECE = 256
MESH = pl.DeviceIdType.MESH


def place():
    me = lax.axis_index("dp")
    return me, me // 32, (me // 8) % 4, (me // 2) % 4, me % 2


def device_at(z, y, x, core):
    return ((z * 4 + y) * 4 + x) * 2 + core


def holder(piece, core):
    line, k = piece // 3, piece % 3
    z, y = line // 4, line % 4
    return device_at(z, y, (k + 8 - y - z) % 4, core)


def held_piece():
    me, z, y, x, core = place()
    k = (x + y + z) % 4
    return (z * 4 + y) * 3 + k, k < 3


def one_hot(mask):
    return jnp.where(mask, 1.0, 0.0).astype(BF)


def swap_rows(outer, inner):
    n = outer * inner
    to = lax.broadcasted_iota(jnp.int32, (n, n), 0)
    source = lax.broadcasted_iota(jnp.int32, (n, n), 1)
    return one_hot(source == lax.rem(to, outer) * inner + lax.div(to, outer))


def pair_kernel(
    lens, ibias, need_ref, q_ref, t_ref, w_hbm, wo_hbm, gain_ref, bias_ref, iw_ref,
    logits_ref, gtext_ref, query_ref, sum_ref,
    x, qkv, tkv, ctx, gh, ga, gc, gqkv, gt, gt_own, prob, own_grad, back, grads,
    table, pieces, held, picked, arrived, back_pieces, back_held, partial, twin_partial,
    totals, back_arrived,
    half_in, in1, sum1, in2, sum2, in3,
    w_ref, wo_ref, load_sem, index_send, index_sem, swap_send, swap_recv,
    partial_send, partial_recv, piece_send, held_sem, pick_send, pick_sem,
    back_send, back_sem, total_send, total_sem,
    half_send, half_recv, s_send, s_recv, a_send, a_recv, twin_send, twin_recv,
):
    rows, width = x.shape
    me, z, y, pos_x, core = place()
    mine, holding = held_piece()
    spots = (pos_x, y, z)
    chips, images = held.shape[1], held.shape[2]
    chip = me // 2
    slots = arrived.shape[1]
    pairs_of_heads = width // 128
    unit = 64
    own = q_ref.shape[0]
    scale = 1.0 / math.sqrt(64.0)
    col = 256
    thirds = range(3)

    def along(axis, step):
        at = [pos_x, y, z]
        at[axis] = (at[axis] + step) % 4
        return device_at(at[2], at[1], at[0], core)

    def axis_of(t, stage):
        return (t + stage) % 3

    twin = me + 1 - 2 * core
    mine_rows = pl.ds(pl.multiple_of(core * 384, 128), 384)
    twin_rows = pl.ds(pl.multiple_of(384 - core * 384, 128), 384)

    def remote(source, target, send, recv, device):
        return pltpu.make_async_remote_copy(
            src_ref=source, dst_ref=target, send_sem=send, recv_sem=recv,
            device_id=(device,), device_id_type=MESH)

    barrier = pltpu.get_barrier_semaphore()

    def greet(device):
        pl.semaphore_signal(barrier, inc=1, device_id=(device,), device_id_type=MESH)

    line = me - me % 8
    for d in range(1, 8):
        greet(line + (me + d) % 8)
    for axis in (1, 2):
        for d in (1, 2, 3):
            greet(along(axis, d))

    w_copy = pltpu.make_async_copy(w_hbm, w_ref, load_sem.at[0])
    wo_copy = pltpu.make_async_copy(wo_hbm, wo_ref, load_sem.at[1])
    w_copy.start()
    wo_copy.start()
    swapped = mm(swap_rows(images, 16), q_ref[...], NN).astype(BF)
    for r in range(16):
        for k in range(3):
            pieces[r * 3 + k] = swapped[r * images : (r + 1) * images, k * PIECE : (k + 1) * PIECE]
    table[me] = need_ref[...]
    pl.semaphore_wait(barrier, 13)

    gathers = []

    def gather(rows, device, number):
        copy = remote(table.at[rows], table.at[rows], index_send.at[number], index_sem.at[number], device)
        copy.start()
        gathers.append(copy)

    def gathered(rows, number):
        pltpu.make_async_copy(table.at[rows], table.at[rows], index_sem.at[number]).wait()

    def tkv_step(j, _):
        c = pl.ds(pl.multiple_of(j * col, col), col)
        cw = pl.ds(pl.multiple_of(j * col + width, col), col)
        tkv[:, c] = mm(t_ref[...], w_ref[:, cw], NN).astype(BF)
        return 0

    def own_step(j, _):
        c = pl.ds(pl.multiple_of(j * col, col), col)
        qkv[0:own, c] = mm(q_ref[...], w_ref[:, c], NN).astype(BF)
        return 0

    for d in range(1, 8):
        gather(pl.ds(me, 1), line + (me + d) % 8, d - 1)
    w_copy.wait()
    lax.fori_loop(0, 6, tkv_step, 0)
    for d in range(1, 8):
        gathered(pl.ds(line + (me + 8 - d) % 8, 1), d - 1)
    for d in (1, 2, 3):
        gather(pl.ds(line, 8), along(1, d), 6 + d)
    lax.fori_loop(0, 5, own_step, 0)
    for d in (1, 2, 3):
        gathered(pl.ds((z * 4 + (y + 4 - d) % 4) * 8, 8), 6 + d)
    for d in (1, 2, 3):
        gather(pl.ds(z * 32, 32), along(2, d), 9 + d)
    lax.fori_loop(5, 9, own_step, 0)
    for d in (1, 2, 3):
        gathered(pl.ds(((z + 4 - d) % 4) * 32, 32), 9 + d)

    def spread(i, _):
        piece = (i + me) % HOLDERS
        target = holder(piece, core)

        @pl.when(target != me)
        def _():
            remote(pieces.at[piece], held.at[core, chip], piece_send, held_sem, target).start()

        @pl.when(target == me)
        def _():
            pltpu.make_async_copy(pieces.at[piece], held.at[core, chip], held_sem).start()

        return 0

    lax.fori_loop(0, HOLDERS, spread, 0)
    other = 1 - core

    def swap_copy():
        return remote(held.at[core], held.at[core], swap_send, swap_recv, twin)

    lane = lax.broadcasted_iota(jnp.int32, (1, 128), 1)
    low = lane < 64

    def by_head(a):
        zero = jnp.zeros_like(a)
        return jnp.concatenate([jnp.where(low, a, zero), jnp.where(low, zero, a)], axis=0)

    def spans(negative, u):
        if negative:
            return pl.ds(pl.multiple_of(own + u * unit, 64), unit), pl.ds(pl.multiple_of(u * 32, 32), 32)
        at = pl.ds(pl.multiple_of(u * unit, 64), unit)
        return at, at

    def keys_of(negative, u, j, first):
        r, tr = spans(negative, u)
        parts = [
            qkv[r, first + j * 128 : first + (j + 1) * 128],
            tkv[tr, first - width + j * 128 : first - width + (j + 1) * 128],
        ]
        if negative:
            parts.append(jnp.zeros((32, 128), BF))
        return by_head(jnp.concatenate(parts, axis=0))

    def forward(negative, u):
        r, _ = spans(negative, u)
        rowi = lax.broadcasted_iota(jnp.int32, (unit, 128), 0)
        lanei = lax.broadcasted_iota(jnp.int32, (unit, 128), 1)
        block = rowi - lax.rem(rowi, 16)
        if negative:
            first = rowi < 32
            start = jnp.where(first, 64, 80)
            live = jnp.where(first, lens[2 * u], lens[2 * u + 1])
        else:
            start = block + 64
            live = jnp.where(
                rowi < 32,
                jnp.where(rowi < 16, lens[4 * u], lens[4 * u + 1]),
                jnp.where(rowi < 48, lens[4 * u + 2], lens[4 * u + 3]),
            )
        valid = ((lanei >= block) & (lanei < block + 16)) | ((lanei >= start) & (lanei < start + live))
        heads = range(pairs_of_heads)
        scores = [
            mm(qkv[r, j * 128 : (j + 1) * 128], keys_of(negative, u, j, width), NT) * scale for j in heads
        ]
        probs = []
        for s in scores:
            parts = []
            for h in range(2):
                sh = jnp.where(valid, s[:, h * 128 : (h + 1) * 128], -1e30)
                e = jnp.exp(sh - jnp.max(sh, axis=-1, keepdims=True))
                parts.append(e * (1.0 / jnp.sum(e, axis=-1, keepdims=True)))
            probs.append(jnp.concatenate(parts, axis=1))
        outs = [mm(p.astype(BF), keys_of(negative, u, j, 2 * width), NN) for j, p in zip(heads, probs)]
        for j, p, o in zip(heads, probs, outs):
            prob[r, j * 256 : (j + 1) * 256] = p
            ctx[r, j * 128 : (j + 1) * 128] = o.astype(BF)

    gain = gain_ref[...].reshape(1, -1)
    bias = bias_ref[...].reshape(1, -1)
    gw0 = gain * iw_ref[0:1, :]
    gw1 = gain * iw_ref[1:2, :]
    slope = (gw1 - gw0) * (1.0 / 16.0)
    slope_mean = jnp.mean(slope)
    base0 = jnp.sum(bias * iw_ref[0:1, :]) + ibias[0]
    base1 = jnp.sum(bias * iw_ref[1:2, :]) + ibias[1]
    part = 256
    tails = part // 16

    def tail(negative, m):
        first = m * part
        r = pl.ds(pl.multiple_of(first, 256), part)
        h = x[r, :].astype(F32) + mm(ctx[r, :], wo_ref[...], NN)
        center = h - jnp.mean(h, axis=-1, keepdims=True)
        spread = jnp.mean(center * center, axis=-1, keepdims=True)
        rstd = lax.rsqrt(spread + 1e-6)
        xhat = center * rstd
        a0 = jnp.sum(xhat * gw0, axis=-1, keepdims=True)
        a1 = jnp.sum(xhat * gw1, axis=-1, keepdims=True)
        l0 = jnp.mean(a0.reshape(tails, 16, 1), axis=1, keepdims=True) + base0
        l1 = jnp.mean(a1.reshape(tails, 16, 1), axis=1, keepdims=True) + base1
        sign = 1.0 if negative else -1.0
        g1 = sign / (1.0 + jnp.exp(-sign * (l1 - l0)))
        g1 = jnp.broadcast_to(g1, (tails, 16, 1)).reshape(part, 1)
        moved = (a1 - a0) * (1.0 / (16.0 * width))
        g = (rstd * g1) * ((slope - slope_mean) - xhat * moved)
        gh[r, :] = g
        low_g = g.astype(BF)
        ga[r, :] = low_g
        gc[r, :] = mm(low_g, wo_ref[...], NT).astype(BF)
        both = jnp.where(lax.broadcasted_iota(jnp.int32, (tails, 1, 128), 2) == 0, l0, l1)
        logits_ref[pl.ds(m * tails, tails)] = both

    def backward(negative, u):
        r, tr = spans(negative, u)
        heads = range(pairs_of_heads)
        cols = [slice(j * 128, (j + 1) * 128) for j in heads]
        gps = [mm(gc[r, c], keys_of(negative, u, j, 2 * width), NT) for j, c in zip(heads, cols)]
        both = []
        for j, gp in zip(heads, gps):
            p = prob[r, j * 256 : (j + 1) * 256]
            gs, lows = [], []
            for h in range(2):
                ph = p[:, h * 128 : (h + 1) * 128]
                gph = gp[:, h * 128 : (h + 1) * 128]
                mean = jnp.sum(gph * ph, axis=-1, keepdims=True)
                gs.append((ph * (gph - mean) * scale).astype(BF))
                lows.append(ph.astype(BF))
            both.append((gs, lows))
        gqs = [mm(jnp.concatenate(gs, axis=1), keys_of(negative, u, j, width), NN) for j, (gs, _) in zip(heads, both)]
        gks = [mm(jnp.concatenate(gs, axis=0), by_head(qkv[r, c]), TN) for c, (gs, _) in zip(cols, both)]
        gvs = [mm(jnp.concatenate(lows, axis=0), by_head(gc[r, c]), TN) for c, (_, lows) in zip(cols, both)]
        for j, c, gq, gk, gv in zip(heads, cols, gqs, gks, gvs):
            cv = slice(width + j * 128, width + (j + 1) * 128)
            gqkv[r, c] = gq.astype(BF)
            gqkv[r, cv] = gk[:64].astype(BF)
            gqkv[r, 2 * width + j * 128 : 2 * width + (j + 1) * 128] = gv[:64].astype(BF)
            if negative:
                gt[tr, c] = (gk[64:96] + gt_own[tr, c]).astype(BF)
                gt[tr, cv] = (gv[64:96] + gt_own[tr, cv]).astype(BF)
            else:
                gt_own[tr, c] = gk[64:]
                gt_own[tr, cv] = gv[64:]

    def loop(first, last, step):
        def body(i, _):
            step(i)
            return 0

        lax.fori_loop(first, last, body, 0)

    def to_rows(m):
        r = pl.ds(pl.multiple_of(m * part, 256), part)
        return mm(gqkv[r, :], w_ref[...], NT) + gh[r, :]

    x[0:own, :] = q_ref[...]
    loop(0, own // unit, lambda u: forward(False, u))

    @pl.when(holding)
    def _():
        pltpu.make_async_copy(held.at[core], held.at[core], held_sem).wait()
        swap_copy().start()
        lanes = lax.broadcasted_iota(jnp.int32, (slots, 128), 1)
        lines = lax.broadcasted_iota(jnp.int32, (slots, 128), 0)
        spot = lax.broadcasted_iota(jnp.int32, (1, 2048), 1)
        side, rest = lax.div(spot, 1024), lax.rem(spot, 1024)
        ids = ((lax.div(rest, 16) * 2 + side) * 16 + lax.rem(rest, 16) + 1).astype(F32)
        values = held.reshape(2048, PIECE)
        pltpu.make_async_copy(held.at[other], held.at[other], swap_recv).wait()

        def pick(g, _):
            columns = []
            for b in range(8):
                row = table[2 * (g * 8 + b) + core].astype(F32)
                eye = lanes == lines + 32 * (b % 4)
                columns.append(jnp.sum(jnp.where(eye, row, 0.0), axis=-1, keepdims=True))
            hot = one_hot(jnp.concatenate(columns, axis=0) == ids)
            chosen = mm(hot, values[...], NN).astype(BF)
            for b in range(8):
                to = g * 8 + b
                target = 2 * to + core
                picked[to] = chosen[b * slots : (b + 1) * slots]

                @pl.when(target != me)
                def _():
                    remote(picked.at[to], arrived.at[mine], pick_send, pick_sem, target).start()

                @pl.when(target == me)
                def _():
                    pltpu.make_async_copy(picked.at[to], arrived.at[mine], pick_sem).start()

            return 0

        lax.fori_loop(0, chips // 8, pick, 0)

    wo_copy.wait()
    loop(0, own // part, lambda m: tail(False, m))
    loop(0, own // unit, lambda u: backward(False, u))
    own_grad[...] = to_rows(0)

    swap = swap_rows(16, slots)
    pltpu.make_async_copy(arrived, arrived, pick_sem).wait()
    for k in range(3):
        c = slice(k * PIECE, (k + 1) * PIECE)
        stacked = jnp.concatenate([arrived[r * 3 + k] for r in range(16)], axis=0)
        x[own:rows, c] = mm(swap, stacked, NN).astype(BF)

    def negative_step(j):
        c = pl.ds(pl.multiple_of(j * col, col), col)
        qkv[own:rows, c] = mm(x[own:rows, :], w_ref[:, c], NN).astype(BF)

    loop(0, 3 * width // col, negative_step)
    loop(0, (rows - own) // unit, lambda u: forward(True, u))
    loop(own // part, rows // part, lambda m: tail(True, m))
    loop(0, (rows - own) // unit, lambda u: backward(True, u))

    def negative_rows(m):
        back[pl.ds(pl.multiple_of((m - 1) * part, 256), part), :] = to_rows(m).astype(BF)

    loop(own // part, rows // part, negative_rows)
    swapped = mm(swap_rows(slots, 16), back[...], NN).astype(BF)
    for r in range(16):
        for k in range(3):
            back_pieces[r * 3 + k] = swapped[r * slots : (r + 1) * slots, k * PIECE : (k + 1) * PIECE]

    def spread_back(i, _):
        piece = (i + me) % HOLDERS
        target = holder(piece, core)

        @pl.when(target != me)
        def _():
            remote(back_pieces.at[piece], back_held.at[chip], back_send, back_sem, target).start()

        @pl.when(target == me)
        def _():
            pltpu.make_async_copy(back_pieces.at[piece], back_held.at[chip], back_sem).start()

        return 0

    lax.fori_loop(0, HOLDERS, spread_back, 0)

    def half_copy(j):
        return remote(grads.at[j, twin_rows], half_in.at[j], half_send.at[j], half_recv.at[j], twin)

    def weight_step(j, _):
        c = pl.ds(pl.multiple_of(j * col, col), col)
        grads[j] = mm(x[...], gqkv[:, c], TN).astype(BF)
        half_copy(j).start()
        return 0

    lax.fori_loop(0, width // col, weight_step, 0)

    def weight_text_step(j, _):
        c = pl.ds(pl.multiple_of(j * col, col), col)
        ct = pl.ds(pl.multiple_of(j * col - width, col), col)
        grads[j] = (mm(x[...], gqkv[:, c], TN) + mm(t_ref[...], gt[:, ct], TN)).astype(BF)
        half_copy(j).start()
        return 0

    lax.fori_loop(width // col, 3 * width // col, weight_text_step, 0)

    def out_step(j, _):
        c = pl.ds(pl.multiple_of(j * col - 3 * width, col), col)
        grads[j] = mm(ctx[...], ga[:, c], TN).astype(BF)
        half_copy(j).start()
        return 0

    lax.fori_loop(3 * width // col, 4 * width // col, out_step, 0)

    sends = []

    def start(copy):
        copy.start()
        sends.append(copy)

    one = {}
    for t in thirds:
        axis = axis_of(t, 0)

        def add_half(k, _, t=t):
            half_copy(4 * t + k).wait_recv()
            own = grads[4 * t + k, mine_rows, :].astype(F32)
            half_in[4 * t + k] = (own + half_in[4 * t + k].astype(F32)).astype(BF)
            return 0

        lax.fori_loop(0, 4, add_half, 0)
        for d in (1, 2, 3):
            to = (spots[axis] + d) % 4
            one[t, d] = remote(half_in.at[4 * t + to], in1.at[t, d - 1],
                               s_send.at[t, d], s_recv.at[t, d], along(axis, d))
            start(one[t, d])

    def partial_copy():
        return remote(partial, twin_partial, partial_send, partial_recv, twin)

    @pl.when(holding)
    def _():
        pltpu.make_async_copy(back_held, back_held, back_sem).wait()
        values = back_held.reshape(chips * slots, PIECE)
        line_at = lax.broadcasted_iota(jnp.int32, (256, 128), 0)
        ids = (lax.div(line_at, 16) * 32 + lax.rem(line_at, 16) + 1).astype(F32)
        rows_of = [
            sum(table[2 * (4 * b + i) + core].astype(F32) for i in range(4)) for b in range(chips // 4)
        ]

        def total_of(g, side):
            shift = (g * 512 + side * 16).astype(F32)
            hot = jnp.concatenate([one_hot(ids == row - shift) for row in rows_of], axis=1)
            return mm(hot, values[...], NN)

        def for_twin(g, _):
            total = total_of(g, other).astype(BF)
            for b in range(16):
                partial[g * 16 + b] = total[b * images : (b + 1) * images]
            return 0

        lax.fori_loop(0, chips // 16, for_twin, 0)
        partial_copy().start()
        partial_copy().wait_recv()

        def add_up(g, _):
            more = twin_partial[pl.ds(g * 16, 16)].reshape(256, PIECE).astype(F32)
            total = (total_of(g, core) + more).astype(BF)
            for b in range(16):
                to = g * 16 + b
                target = 2 * to + core
                totals[to] = total[b * images : (b + 1) * images]

                @pl.when(target != me)
                def _():
                    remote(totals.at[to], back_arrived.at[mine], total_send, total_sem, target).start()

                @pl.when(target == me)
                def _():
                    pltpu.make_async_copy(totals.at[to], back_arrived.at[mine], total_sem).start()

            return 0

        lax.fori_loop(0, chips // 16, add_up, 0)

    gtext_ref[...] = mm(gt[...], w_ref[:, width:], NT).astype(BF)

    two = {}
    for t in thirds:
        axis, after = axis_of(t, 0), axis_of(t, 1)
        for d in (1, 2, 3):
            one[t, d].wait_recv()
        total = half_in[4 * t + spots[axis]].astype(F32)
        for d in range(3):
            total += in1[t, d].astype(F32)
        sum1[t] = total.astype(BF)
        for d in (1, 2, 3):
            to = (spots[after] + d) % 4
            two[t, d] = remote(sum1.at[t, pl.ds(pl.multiple_of(to * 96, 32), 96)], in2.at[t, d - 1],
                               s_send.at[t, 3 + d], s_recv.at[t, 3 + d], along(after, d))
            start(two[t, d])

    def corner(ref, first, spot):
        rows = pl.ds(pl.multiple_of(first + (spot // 2) * 48, 16), 48)
        return ref.at[rows, pl.ds(pl.multiple_of((spot % 2) * 128, 128), 128)]

    three = {}
    for t in thirds:
        axis, after = axis_of(t, 1), axis_of(t, 2)
        for d in (1, 2, 3):
            two[t, d].wait_recv()
        total = sum1[t, pl.ds(pl.multiple_of(spots[axis] * 96, 32), 96), :].astype(F32)
        for d in range(3):
            total += in2[t, d].astype(F32)
        sum2[t] = total.astype(BF)
        for d in (1, 2, 3):
            to = (spots[after] + d) % 4
            three[t, d] = remote(corner(sum2.at[t], 0, to), in3.at[t, d - 1],
                                 s_send.at[t, 6 + d], s_recv.at[t, 6 + d], along(after, d))
            start(three[t, d])

    last = {}
    for t in thirds:
        axis = axis_of(t, 2)
        for d in (1, 2, 3):
            three[t, d].wait_recv()
        total = corner(sum2.at[t], 0, spots[axis])[...].astype(F32)
        for d in range(3):
            total += in3[t, d].astype(F32)
        block = sum_ref.at[4 * t + spots[axis_of(t, 0)]]
        first = core * 384 + spots[axis_of(t, 1)] * 96
        piece = corner(block, first, spots[axis])
        piece[...] = total.astype(BF)
        for d in (1, 2, 3):
            last[t, d] = remote(piece, piece, a_send.at[t, d], a_recv.at[t, d], along(axis, d))
            start(last[t, d])

    def came(t, stage, ref, d):
        return pltpu.make_async_copy(ref, ref, a_recv.at[t, stage * 3 + d])

    for t in thirds:
        axis = axis_of(t, 1)
        block = sum_ref.at[4 * t + spots[axis_of(t, 0)]]
        first = core * 384 + spots[axis] * 96
        for d in (1, 2, 3):
            came(t, 0, corner(block, first, (spots[axis_of(t, 2)] + 4 - d) % 4), d).wait()
        piece = block.at[pl.ds(pl.multiple_of(first, 32), 96)]
        for d in (1, 2, 3):
            start(remote(piece, piece, a_send.at[t, 3 + d], a_recv.at[t, 3 + d], along(axis, d)))

    for t in thirds:
        axis = axis_of(t, 0)
        block = sum_ref.at[4 * t + spots[axis]]
        for d in (1, 2, 3):
            spot = (spots[axis_of(t, 1)] + 4 - d) % 4
            came(t, 1, block.at[pl.ds(pl.multiple_of(core * 384 + spot * 96, 32), 96)], d).wait()
        piece = block.at[mine_rows]
        start(remote(piece, piece, twin_send.at[t, 0], twin_recv.at[t, 0], twin))
        for d in (1, 2, 3):
            start(remote(piece, piece, a_send.at[t, 6 + d], a_recv.at[t, 6 + d], along(axis, d)))

    for t in thirds:
        axis = axis_of(t, 0)
        for d in (1, 2, 3):
            piece = sum_ref.at[4 * t + (spots[axis] + 4 - d) % 4, mine_rows]
            came(t, 2, piece, d).wait()
            start(remote(piece, piece, twin_send.at[t, d], twin_recv.at[t, d], twin))


    pltpu.make_async_copy(back_arrived, back_arrived, total_sem).wait()
    swap = swap_rows(16, images)
    for k in range(3):
        c = slice(k * PIECE, (k + 1) * PIECE)
        stacked = jnp.concatenate([back_arrived[r * 3 + k] for r in range(16)], axis=0)
        query_ref[:, c] = (own_grad[:, c] + mm(swap, stacked, NN)).astype(BF)

    for t in thirds:
        for d in range(4):
            late = sum_ref.at[4 * t + (spots[axis_of(t, 0)] + 4 - d) % 4, twin_rows]
            pltpu.make_async_copy(late, late, twin_recv.at[t, d]).wait()
    for copy in sends:
        copy.wait_send()

    def half_sent(j, _):
        half_copy(j).wait_send()
        return 0

    lax.fori_loop(0, 4 * width // col, half_sent, 0)

    def sent(ref, count, semaphore):
        pltpu.make_async_copy(ref.at[0:count], ref.at[0:count], semaphore).wait()

    for copy in gathers:
        copy.wait_send()

    @pl.when(holding)
    def _():
        swap_copy().wait_send()
        partial_copy().wait_send()
        sent(pieces, HOLDERS - 1, piece_send)
        sent(picked, chips - 1, pick_send)
        sent(back_pieces, HOLDERS - 1, back_send)
        sent(totals, chips - 1, total_send)

    @pl.when(jnp.logical_not(holding))
    def _():
        sent(pieces, HOLDERS, piece_send)
        sent(back_pieces, HOLDERS, back_send)


def pair_losses(lens, ib, need, queries, texts, w, wo, gain, bias, iw, peers):
    own, width = queries.shape
    rows, trows = 3 * own, texts.shape[0]
    images = own // 16
    vmem = pl.BlockSpec(memory_space=pltpu.VMEM)
    smem = pl.BlockSpec(memory_space=pltpu.SMEM)
    shape = jax.ShapeDtypeStruct
    dma = pltpu.SemaphoreType.DMA
    return pl.pallas_call(
        pair_kernel,
        out_shape=(
            shape((rows // 16, 1, 128), F32),
            shape((trows, width), BF),
            shape((own, width), BF),
            shape((12, width, 256), BF),
        ),
        in_specs=[smem, smem] + [vmem] * 3 + [pl.BlockSpec(memory_space=pl.ANY)] * 2 + [vmem] * 3,
        out_specs=(vmem,) * 4,
        scratch_shapes=[
            pltpu.VMEM((rows, width), BF),
            pltpu.VMEM((rows, 3 * width), BF),
            pltpu.VMEM((trows, 2 * width), BF),
            pltpu.VMEM((rows, width), BF),
            pltpu.VMEM((rows, width), F32),
            pltpu.VMEM((rows, width), BF),
            pltpu.VMEM((rows, width), BF),
            pltpu.VMEM((rows, 3 * width), BF),
            pltpu.VMEM((trows, 2 * width), BF),
            pltpu.VMEM((trows, 2 * width), F32),
            pltpu.VMEM((rows, 2 * width), F32),
            pltpu.VMEM((own, width), F32),
            pltpu.VMEM((2 * own, width), BF),
            pltpu.VMEM((12, width, 256), BF),
            pltpu.VMEM((peers, 1, 128), jnp.int32),
            pltpu.VMEM((HOLDERS, images, PIECE), BF),
            pltpu.VMEM((2, peers // 2, images, PIECE), BF),
            pltpu.VMEM((peers // 2, 2 * images, PIECE), BF),
            pltpu.VMEM((HOLDERS, 2 * images, PIECE), BF),
            pltpu.VMEM((HOLDERS, 2 * images, PIECE), BF),
            pltpu.VMEM((peers // 2, 2 * images, PIECE), BF),
            pltpu.VMEM((peers // 2, images, PIECE), BF),
            pltpu.VMEM((peers // 2, images, PIECE), BF),
            pltpu.VMEM((peers // 2, images, PIECE), BF),
            pltpu.VMEM((HOLDERS, images, PIECE), BF),
            pltpu.VMEM((12, 384, 256), BF),
            pltpu.VMEM((3, 3, 384, 256), BF),
            pltpu.VMEM((3, 384, 256), BF),
            pltpu.VMEM((3, 3, 96, 256), BF),
            pltpu.VMEM((3, 96, 256), BF),
            pltpu.VMEM((3, 3, 48, 128), BF),
            pltpu.VMEM((width, 3 * width), BF),
            pltpu.VMEM((width, width), BF),
            dma((2,)), dma((13,)), dma((13,)), dma, dma, dma, dma,
            dma, dma, dma, dma, dma, dma, dma, dma,
            dma((12,)), dma((12,)), dma((3, 10)), dma((3, 10)), dma((3, 10)), dma((3, 10)),
            dma((3, 4)), dma((3, 4)),
        ],
        compiler_params=pltpu.CompilerParams(
            vmem_limit_bytes=63 * 1024 * 1024, has_side_effects=True, collective_id=0
        ),
        name="pair_losses",
    )(lens, ib, need, queries, texts, w, wo, gain, bias, iw.T)


def widen_kernel(share, sum_ref, qkv_ref, out_ref):
    for j in range(12):
        block = sum_ref[j].astype(F32) * share
        if j < 9:
            qkv_ref[:, j * 256 : (j + 1) * 256] = block
        else:
            out_ref[:, (j - 9) * 256 : (j - 8) * 256] = block


def widen(sums, share):
    width, part = sums.shape[1], 96
    return pl.pallas_call(
        lambda *refs: widen_kernel(share, *refs),
        grid=(width // part,),
        out_shape=(
            jax.ShapeDtypeStruct((width, 3 * width), F32),
            jax.ShapeDtypeStruct((width, width), F32),
        ),
        in_specs=[pl.BlockSpec((12, part, 256), lambda j: (0, j, 0))],
        out_specs=(
            pl.BlockSpec((part, 3 * width), lambda j: (j, 0)),
            pl.BlockSpec((part, width), lambda j: (j, 0)),
        ),
        name="widen",
    )(sums)


def on_device(
    text_states, text_len, query_states, neg_owner, neg_slot,
    projection_weight, output_weight, ln_gain, ln_bias, itm_weight, itm_bias,
):
    captions, query_rows, width = query_states.shape
    peers = lax.axis_size("dp")
    me = lax.axis_index("dp")
    wanted = (captions * neg_owner + neg_slot + 1).reshape(1, 2 * captions)
    group = jnp.arange(4)[:, None] == me // 2 % 4
    need = jnp.where(group, wanted, 0).reshape(1, 128)
    logits, grad_text, grad_query, sums = pair_losses(
        text_len, itm_bias, need, query_states.reshape(-1, width), text_states.reshape(-1, width),
        projection_weight, output_weight, ln_gain, ln_bias, itm_weight, peers,
    )
    sum_qkv, sum_out = widen(sums, 1.0 / (captions * peers))
    return (
        jnp.concatenate(
            [logits[:captions, 0, :2].reshape(captions, 1, 2), logits[captions:, 0, :2].reshape(captions, 2, 2)],
            axis=1,
        ),
        grad_text.reshape(text_states.shape),
        grad_query.reshape(query_states.shape),
        sum_qkv,
        sum_out,
    )


def solution(mesh):
    rows = P("dp", None, None)
    placed = (rows, P("dp"), rows, P("dp", None), P("dp", None)) + (P(),) * 6
    return jax.shard_map(
        on_device, mesh=mesh, in_specs=placed, out_specs=(rows, rows, rows, P(), P()), check_vma=False
    )
```

```python
import math
import jax
import jax.numpy as jnp
from jax import lax
from jax.experimental import pallas as pl
from jax.experimental.pallas import tpu as pltpu
from jax.sharding import PartitionSpec as P

F32 = jnp.float32
BF = jnp.bfloat16
NN = (((1,), (0,)), ((), ()))
NT = (((1,), (1,)), ((), ()))
TN = (((0,), (0,)), ((), ()))


def mm(a, b, dims):
    return lax.dot_general(a, b, dims, preferred_element_type=F32)


HOLDERS = 48
PIECE = 256
MESH = pl.DeviceIdType.MESH


def place():
    me = lax.axis_index("dp")
    return me, me // 32, (me // 8) % 4, (me // 2) % 4, me % 2


def device_at(z, y, x, core):
    return ((z * 4 + y) * 4 + x) * 2 + core


def holder(piece, core):
    line, k = piece // 3, piece % 3
    z, y = line // 4, line % 4
    return device_at(z, y, (k + 8 - y - z) % 4, core)


def held_piece():
    me, z, y, x, core = place()
    k = (x + y + z) % 4
    return (z * 4 + y) * 3 + k, k < 3


def one_hot(mask):
    return jnp.where(mask, 1.0, 0.0).astype(BF)


def swap_rows(outer, inner):
    n = outer * inner
    to = lax.broadcasted_iota(jnp.int32, (n, n), 0)
    source = lax.broadcasted_iota(jnp.int32, (n, n), 1)
    return one_hot(source == lax.rem(to, outer) * inner + lax.div(to, outer))


def pair_kernel(
    lens, ibias, need_ref, q_ref, t_ref, w_hbm, wo_hbm, gain_ref, bias_ref, iw_ref,
    logits_ref, gtext_ref, query_ref, sum_ref,
    x, qkv, tkv, ctx, gh, ga, gc, gqkv, gt, gt_own, prob, own_grad, back, grads,
    table, pieces, held, picked, arrived, back_pieces, back_held, partial, twin_partial,
    totals, back_arrived,
    half_in, in1, sum1, in2, sum2, in3,
    w_ref, wo_ref, load_sem, index_send, index_sem, swap_send, swap_recv,
    partial_send, partial_recv, piece_send, held_sem, pick_send, pick_sem,
    back_send, back_sem, total_send, total_sem,
    half_send, half_recv, s_send, s_recv, a_send, a_recv, twin_send, twin_recv,
):
    rows, width = x.shape
    me, z, y, pos_x, core = place()
    mine, holding = held_piece()
    spots = (pos_x, y, z)
    chips, images = held.shape[1], held.shape[2]
    chip = me // 2
    slots = arrived.shape[1]
    pairs_of_heads = width // 128
    unit = 64
    own = q_ref.shape[0]
    scale = 1.0 / math.sqrt(64.0)
    col = 256
    thirds = range(3)

    def along(axis, step):
        at = [pos_x, y, z]
        at[axis] = (at[axis] + step) % 4
        return device_at(at[2], at[1], at[0], core)

    def axis_of(t, stage):
        return (t + stage) % 3

    twin = me + 1 - 2 * core
    mine_rows = pl.ds(pl.multiple_of(core * 384, 128), 384)
    twin_rows = pl.ds(pl.multiple_of(384 - core * 384, 128), 384)

    def remote(source, target, send, recv, device):
        return pltpu.make_async_remote_copy(
            src_ref=source, dst_ref=target, send_sem=send, recv_sem=recv,
            device_id=(device,), device_id_type=MESH)

    barrier = pltpu.get_barrier_semaphore()

    def greet(device):
        pl.semaphore_signal(barrier, inc=1, device_id=(device,), device_id_type=MESH)

    line = me - me % 8
    for d in range(1, 8):
        greet(line + (me + d) % 8)
    for axis in (1, 2):
        for d in (1, 2, 3):
            greet(along(axis, d))

    w_copy = pltpu.make_async_copy(w_hbm, w_ref, load_sem.at[0])
    wo_copy = pltpu.make_async_copy(wo_hbm, wo_ref, load_sem.at[1])
    w_copy.start()
    wo_copy.start()
    swapped = mm(swap_rows(images, 16), q_ref[...], NN).astype(BF)
    for r in range(16):
        for k in range(3):
            pieces[r * 3 + k] = swapped[r * images : (r + 1) * images, k * PIECE : (k + 1) * PIECE]
    table[me] = need_ref[...]
    pl.semaphore_wait(barrier, 13)

    gathers = []

    def gather(rows, device, number):
        copy = remote(table.at[rows], table.at[rows], index_send.at[number], index_sem.at[number], device)
        copy.start()
        gathers.append(copy)

    def gathered(rows, number):
        pltpu.make_async_copy(table.at[rows], table.at[rows], index_sem.at[number]).wait()

    def tkv_step(j, _):
        c = pl.ds(pl.multiple_of(j * col, col), col)
        cw = pl.ds(pl.multiple_of(j * col + width, col), col)
        tkv[:, c] = mm(t_ref[...], w_ref[:, cw], NN).astype(BF)
        return 0

    def own_step(j, _):
        c = pl.ds(pl.multiple_of(j * col, col), col)
        qkv[0:own, c] = mm(q_ref[...], w_ref[:, c], NN).astype(BF)
        return 0

    for d in range(1, 8):
        gather(pl.ds(me, 1), line + (me + d) % 8, d - 1)
    w_copy.wait()
    lax.fori_loop(0, 6, tkv_step, 0)
    for d in range(1, 8):
        gathered(pl.ds(line + (me + 8 - d) % 8, 1), d - 1)
    for d in (1, 2, 3):
        gather(pl.ds(line, 8), along(1, d), 6 + d)
    lax.fori_loop(0, 5, own_step, 0)
    for d in (1, 2, 3):
        gathered(pl.ds((z * 4 + (y + 4 - d) % 4) * 8, 8), 6 + d)
    for d in (1, 2, 3):
        gather(pl.ds(z * 32, 32), along(2, d), 9 + d)
    lax.fori_loop(5, 9, own_step, 0)
    for d in (1, 2, 3):
        gathered(pl.ds(((z + 4 - d) % 4) * 32, 32), 9 + d)

    def spread(i, _):
        piece = (i + me) % HOLDERS
        target = holder(piece, core)

        @pl.when(target != me)
        def _():
            remote(pieces.at[piece], held.at[core, chip], piece_send, held_sem, target).start()

        @pl.when(target == me)
        def _():
            pltpu.make_async_copy(pieces.at[piece], held.at[core, chip], held_sem).start()

        return 0

    lax.fori_loop(0, HOLDERS, spread, 0)
    other = 1 - core

    def swap_copy():
        return remote(held.at[core], held.at[core], swap_send, swap_recv, twin)

    lane = lax.broadcasted_iota(jnp.int32, (1, 128), 1)
    low = lane < 64

    def by_head(a):
        zero = jnp.zeros_like(a)
        return jnp.concatenate([jnp.where(low, a, zero), jnp.where(low, zero, a)], axis=0)

    def spans(negative, u):
        if negative:
            return pl.ds(pl.multiple_of(own + u * unit, 64), unit), pl.ds(pl.multiple_of(u * 32, 32), 32)
        at = pl.ds(pl.multiple_of(u * unit, 64), unit)
        return at, at

    def keys_of(negative, u, j, first):
        r, tr = spans(negative, u)
        parts = [
            qkv[r, first + j * 128 : first + (j + 1) * 128],
            tkv[tr, first - width + j * 128 : first - width + (j + 1) * 128],
        ]
        if negative:
            parts.append(jnp.zeros((32, 128), BF))
        return by_head(jnp.concatenate(parts, axis=0))

    def mask_of(negative, u):
        rowi = lax.broadcasted_iota(jnp.int32, (unit, 128), 0)
        lanei = lax.broadcasted_iota(jnp.int32, (unit, 128), 1)
        block = rowi - lax.rem(rowi, 16)
        if negative:
            first = rowi < 32
            start = jnp.where(first, 64, 80)
            live = jnp.where(first, lens[2 * u], lens[2 * u + 1])
        else:
            start = block + 64
            live = jnp.where(
                rowi < 32,
                jnp.where(rowi < 16, lens[4 * u], lens[4 * u + 1]),
                jnp.where(rowi < 48, lens[4 * u + 2], lens[4 * u + 3]),
            )
        return ((lanei >= block) & (lanei < block + 16)) | ((lanei >= start) & (lanei < start + live))

    def forward(negative, v):
        us = (2 * v, 2 * v + 1)
        heads = [(i, j) for i in range(2) for j in range(pairs_of_heads)]
        rs = [spans(negative, u)[0] for u in us]
        valid = [mask_of(negative, u) for u in us]
        scores = [
            mm(qkv[rs[u], j * 128 : (j + 1) * 128], keys_of(negative, us[u], j, width), NT) * scale for u, j in heads
        ]
        probs = []
        for (u, _), s in zip(heads, scores):
            parts = []
            for h in range(2):
                sh = jnp.where(valid[u], s[:, h * 128 : (h + 1) * 128], -1e30)
                e = jnp.exp(sh - jnp.max(sh, axis=-1, keepdims=True))
                parts.append(e * (1.0 / jnp.sum(e, axis=-1, keepdims=True)))
            probs.append(jnp.concatenate(parts, axis=1))
        outs = [mm(p.astype(BF), keys_of(negative, us[u], j, 2 * width), NN) for (u, j), p in zip(heads, probs)]
        for (u, j), p, o in zip(heads, probs, outs):
            prob[rs[u], j * 256 : (j + 1) * 256] = p
            ctx[rs[u], j * 128 : (j + 1) * 128] = o.astype(BF)

    gain = gain_ref[...].reshape(1, -1)
    bias = bias_ref[...].reshape(1, -1)
    gw0 = gain * iw_ref[0:1, :]
    gw1 = gain * iw_ref[1:2, :]
    slope = (gw1 - gw0) * (1.0 / 16.0)
    slope_mean = jnp.mean(slope)
    base0 = jnp.sum(bias * iw_ref[0:1, :]) + ibias[0]
    base1 = jnp.sum(bias * iw_ref[1:2, :]) + ibias[1]
    part = 256
    tails = part // 16

    def tail(negative, m):
        first = m * part
        r = pl.ds(pl.multiple_of(first, 256), part)
        h = x[r, :].astype(F32) + mm(ctx[r, :], wo_ref[...], NN)
        center = h - jnp.mean(h, axis=-1, keepdims=True)
        spread = jnp.mean(center * center, axis=-1, keepdims=True)
        rstd = lax.rsqrt(spread + 1e-6)
        xhat = center * rstd
        a0 = jnp.sum(xhat * gw0, axis=-1, keepdims=True)
        a1 = jnp.sum(xhat * gw1, axis=-1, keepdims=True)
        l0 = jnp.mean(a0.reshape(tails, 16, 1), axis=1, keepdims=True) + base0
        l1 = jnp.mean(a1.reshape(tails, 16, 1), axis=1, keepdims=True) + base1
        sign = 1.0 if negative else -1.0
        g1 = sign / (1.0 + jnp.exp(-sign * (l1 - l0)))
        g1 = jnp.broadcast_to(g1, (tails, 16, 1)).reshape(part, 1)
        moved = (a1 - a0) * (1.0 / (16.0 * width))
        g = (rstd * g1) * ((slope - slope_mean) - xhat * moved)
        gh[r, :] = g
        low_g = g.astype(BF)
        ga[r, :] = low_g
        gc[r, :] = mm(low_g, wo_ref[...], NT).astype(BF)
        both = jnp.where(lax.broadcasted_iota(jnp.int32, (tails, 1, 128), 2) == 0, l0, l1)
        logits_ref[pl.ds(m * tails, tails)] = both

    def backward(negative, v):
        us = (2 * v, 2 * v + 1)
        heads = [(i, j) for i in range(2) for j in range(pairs_of_heads)]
        rs = [spans(negative, u)[0] for u in us]
        trs = [spans(negative, u)[1] for u in us]
        cols = [slice(j * 128, (j + 1) * 128) for _, j in heads]
        gps = [mm(gc[rs[u], c], keys_of(negative, us[u], j, 2 * width), NT) for (u, j), c in zip(heads, cols)]
        both = []
        for (u, j), gp in zip(heads, gps):
            p = prob[rs[u], j * 256 : (j + 1) * 256]
            gs, lows = [], []
            for h in range(2):
                ph = p[:, h * 128 : (h + 1) * 128]
                gph = gp[:, h * 128 : (h + 1) * 128]
                mean = jnp.sum(gph * ph, axis=-1, keepdims=True)
                gs.append((ph * (gph - mean) * scale).astype(BF))
                lows.append(ph.astype(BF))
            both.append((gs, lows))
        gqs = [
            mm(jnp.concatenate(gs, axis=1), keys_of(negative, us[u], j, width), NN)
            for (u, j), (gs, _) in zip(heads, both)
        ]
        gks = [
            mm(jnp.concatenate(gs, axis=0), by_head(qkv[rs[u], c]), TN)
            for (u, _), c, (gs, _) in zip(heads, cols, both)
        ]
        gvs = [
            mm(jnp.concatenate(lows, axis=0), by_head(gc[rs[u], c]), TN)
            for (u, _), c, (_, lows) in zip(heads, cols, both)
        ]
        for (u, j), c, gq, gk, gv in zip(heads, cols, gqs, gks, gvs):
            r, tr = rs[u], trs[u]
            cv = slice(width + j * 128, width + (j + 1) * 128)
            gqkv[r, c] = gq.astype(BF)
            gqkv[r, cv] = gk[:64].astype(BF)
            gqkv[r, 2 * width + j * 128 : 2 * width + (j + 1) * 128] = gv[:64].astype(BF)
            if negative:
                gt[tr, c] = (gk[64:96] + gt_own[tr, c]).astype(BF)
                gt[tr, cv] = (gv[64:96] + gt_own[tr, cv]).astype(BF)
            else:
                gt_own[tr, c] = gk[64:]
                gt_own[tr, cv] = gv[64:]

    def loop(first, last, step):
        def body(i, _):
            step(i)
            return 0

        lax.fori_loop(first, last, body, 0)

    def to_rows(m):
        r = pl.ds(pl.multiple_of(m * part, 256), part)
        return mm(gqkv[r, :], w_ref[...], NT) + gh[r, :]

    x[0:own, :] = q_ref[...]
    loop(0, own // (2 * unit), lambda v: forward(False, v))

    @pl.when(holding)
    def _():
        pltpu.make_async_copy(held.at[core], held.at[core], held_sem).wait()
        swap_copy().start()
        lanes = lax.broadcasted_iota(jnp.int32, (slots, 128), 1)
        lines = lax.broadcasted_iota(jnp.int32, (slots, 128), 0)
        spot = lax.broadcasted_iota(jnp.int32, (1, 2048), 1)
        side, rest = lax.div(spot, 1024), lax.rem(spot, 1024)
        ids = ((lax.div(rest, 16) * 2 + side) * 16 + lax.rem(rest, 16) + 1).astype(F32)
        values = held.reshape(2048, PIECE)
        pltpu.make_async_copy(held.at[other], held.at[other], swap_recv).wait()

        def pick(g, _):
            columns = []
            for b in range(8):
                row = table[2 * (g * 8 + b) + core].astype(F32)
                eye = lanes == lines + 32 * (b % 4)
                columns.append(jnp.sum(jnp.where(eye, row, 0.0), axis=-1, keepdims=True))
            hot = one_hot(jnp.concatenate(columns, axis=0) == ids)
            chosen = mm(hot, values[...], NN).astype(BF)
            for b in range(8):
                to = g * 8 + b
                target = 2 * to + core
                picked[to] = chosen[b * slots : (b + 1) * slots]

                @pl.when(target != me)
                def _():
                    remote(picked.at[to], arrived.at[mine], pick_send, pick_sem, target).start()

                @pl.when(target == me)
                def _():
                    pltpu.make_async_copy(picked.at[to], arrived.at[mine], pick_sem).start()

            return 0

        lax.fori_loop(0, chips // 8, pick, 0)

    wo_copy.wait()
    loop(0, own // part, lambda m: tail(False, m))
    loop(0, own // (2 * unit), lambda v: backward(False, v))
    own_grad[...] = to_rows(0)

    swap = swap_rows(16, slots)
    pltpu.make_async_copy(arrived, arrived, pick_sem).wait()
    for k in range(3):
        c = slice(k * PIECE, (k + 1) * PIECE)
        stacked = jnp.concatenate([arrived[r * 3 + k] for r in range(16)], axis=0)
        x[own:rows, c] = mm(swap, stacked, NN).astype(BF)

    def negative_step(j):
        c = pl.ds(pl.multiple_of(j * col, col), col)
        qkv[own:rows, c] = mm(x[own:rows, :], w_ref[:, c], NN).astype(BF)

    loop(0, 3 * width // col, negative_step)
    loop(0, (rows - own) // (2 * unit), lambda v: forward(True, v))
    loop(own // part, rows // part, lambda m: tail(True, m))
    loop(0, (rows - own) // (2 * unit), lambda v: backward(True, v))

    def negative_rows(m):
        back[pl.ds(pl.multiple_of((m - 1) * part, 256), part), :] = to_rows(m).astype(BF)

    loop(own // part, rows // part, negative_rows)
    swapped = mm(swap_rows(slots, 16), back[...], NN).astype(BF)
    for r in range(16):
        for k in range(3):
            back_pieces[r * 3 + k] = swapped[r * slots : (r + 1) * slots, k * PIECE : (k + 1) * PIECE]

    def spread_back(i, _):
        piece = (i + me) % HOLDERS
        target = holder(piece, core)

        @pl.when(target != me)
        def _():
            remote(back_pieces.at[piece], back_held.at[chip], back_send, back_sem, target).start()

        @pl.when(target == me)
        def _():
            pltpu.make_async_copy(back_pieces.at[piece], back_held.at[chip], back_sem).start()

        return 0

    lax.fori_loop(0, HOLDERS, spread_back, 0)

    def half_copy(j):
        return remote(grads.at[j, twin_rows], half_in.at[j], half_send.at[j], half_recv.at[j], twin)

    def weight_step(j, _):
        c = pl.ds(pl.multiple_of(j * col, col), col)
        grads[j] = mm(x[...], gqkv[:, c], TN).astype(BF)
        half_copy(j).start()
        return 0

    lax.fori_loop(0, width // col, weight_step, 0)

    def weight_text_step(j, _):
        c = pl.ds(pl.multiple_of(j * col, col), col)
        ct = pl.ds(pl.multiple_of(j * col - width, col), col)
        grads[j] = (mm(x[...], gqkv[:, c], TN) + mm(t_ref[...], gt[:, ct], TN)).astype(BF)
        half_copy(j).start()
        return 0

    lax.fori_loop(width // col, 3 * width // col, weight_text_step, 0)

    def out_step(j, _):
        c = pl.ds(pl.multiple_of(j * col - 3 * width, col), col)
        grads[j] = mm(ctx[...], ga[:, c], TN).astype(BF)
        half_copy(j).start()
        return 0

    lax.fori_loop(3 * width // col, 4 * width // col, out_step, 0)

    sends = []

    def start(copy):
        copy.start()
        sends.append(copy)

    one = {}
    for t in thirds:
        axis = axis_of(t, 0)

        def add_half(k, _, t=t):
            half_copy(4 * t + k).wait_recv()
            own = grads[4 * t + k, mine_rows, :].astype(F32)
            half_in[4 * t + k] = (own + half_in[4 * t + k].astype(F32)).astype(BF)
            return 0

        lax.fori_loop(0, 4, add_half, 0)
        for d in (1, 2, 3):
            to = (spots[axis] + d) % 4
            one[t, d] = remote(half_in.at[4 * t + to], in1.at[t, d - 1],
                               s_send.at[t, d], s_recv.at[t, d], along(axis, d))
            start(one[t, d])

    def partial_copy():
        return remote(partial, twin_partial, partial_send, partial_recv, twin)

    @pl.when(holding)
    def _():
        pltpu.make_async_copy(back_held, back_held, back_sem).wait()
        values = back_held.reshape(chips * slots, PIECE)
        line_at = lax.broadcasted_iota(jnp.int32, (256, 128), 0)
        ids = (lax.div(line_at, 16) * 32 + lax.rem(line_at, 16) + 1).astype(F32)
        rows_of = [
            sum(table[2 * (4 * b + i) + core].astype(F32) for i in range(4)) for b in range(chips // 4)
        ]

        def total_of(g, side):
            shift = (g * 512 + side * 16).astype(F32)
            hot = jnp.concatenate([one_hot(ids == row - shift) for row in rows_of], axis=1)
            return mm(hot, values[...], NN)

        def for_twin(g, _):
            total = total_of(g, other).astype(BF)
            for b in range(16):
                partial[g * 16 + b] = total[b * images : (b + 1) * images]
            return 0

        lax.fori_loop(0, chips // 16, for_twin, 0)
        partial_copy().start()

    gtext_ref[...] = mm(gt[...], w_ref[:, width:], NT).astype(BF)

    two = {}
    for t in thirds:
        axis, after = axis_of(t, 0), axis_of(t, 1)
        for d in (1, 2, 3):
            one[t, d].wait_recv()
        total = half_in[4 * t + spots[axis]].astype(F32)
        for d in range(3):
            total += in1[t, d].astype(F32)
        sum1[t] = total.astype(BF)
        for d in (1, 2, 3):
            to = (spots[after] + d) % 4
            two[t, d] = remote(sum1.at[t, pl.ds(pl.multiple_of(to * 96, 32), 96)], in2.at[t, d - 1],
                               s_send.at[t, 3 + d], s_recv.at[t, 3 + d], along(after, d))
            start(two[t, d])

    def corner(ref, first, spot):
        rows = pl.ds(pl.multiple_of(first + (spot // 2) * 48, 16), 48)
        return ref.at[rows, pl.ds(pl.multiple_of((spot % 2) * 128, 128), 128)]

    three = {}
    for t in thirds:
        axis, after = axis_of(t, 1), axis_of(t, 2)
        for d in (1, 2, 3):
            two[t, d].wait_recv()
        total = sum1[t, pl.ds(pl.multiple_of(spots[axis] * 96, 32), 96), :].astype(F32)
        for d in range(3):
            total += in2[t, d].astype(F32)
        sum2[t] = total.astype(BF)
        for d in (1, 2, 3):
            to = (spots[after] + d) % 4
            three[t, d] = remote(corner(sum2.at[t], 0, to), in3.at[t, d - 1],
                                 s_send.at[t, 6 + d], s_recv.at[t, 6 + d], along(after, d))
            start(three[t, d])

    last = {}
    for t in thirds:
        axis = axis_of(t, 2)
        for d in (1, 2, 3):
            three[t, d].wait_recv()
        total = corner(sum2.at[t], 0, spots[axis])[...].astype(F32)
        for d in range(3):
            total += in3[t, d].astype(F32)
        block = sum_ref.at[4 * t + spots[axis_of(t, 0)]]
        first = core * 384 + spots[axis_of(t, 1)] * 96
        piece = corner(block, first, spots[axis])
        piece[...] = total.astype(BF)
        for d in (1, 2, 3):
            last[t, d] = remote(piece, piece, a_send.at[t, d], a_recv.at[t, d], along(axis, d))
            start(last[t, d])

    def came(t, stage, ref, d):
        return pltpu.make_async_copy(ref, ref, a_recv.at[t, stage * 3 + d])

    for t in thirds:
        axis = axis_of(t, 1)
        block = sum_ref.at[4 * t + spots[axis_of(t, 0)]]
        first = core * 384 + spots[axis] * 96
        for d in (1, 2, 3):
            came(t, 0, corner(block, first, (spots[axis_of(t, 2)] + 4 - d) % 4), d).wait()
        piece = block.at[pl.ds(pl.multiple_of(first, 32), 96)]
        for d in (1, 2, 3):
            start(remote(piece, piece, a_send.at[t, 3 + d], a_recv.at[t, 3 + d], along(axis, d)))

    for t in thirds:
        axis = axis_of(t, 0)
        block = sum_ref.at[4 * t + spots[axis]]
        for d in (1, 2, 3):
            spot = (spots[axis_of(t, 1)] + 4 - d) % 4
            came(t, 1, block.at[pl.ds(pl.multiple_of(core * 384 + spot * 96, 32), 96)], d).wait()
        piece = block.at[mine_rows]
        start(remote(piece, piece, twin_send.at[t, 0], twin_recv.at[t, 0], twin))
        for d in (1, 2, 3):
            start(remote(piece, piece, a_send.at[t, 6 + d], a_recv.at[t, 6 + d], along(axis, d)))

    @pl.when(holding)
    def _():
        partial_copy().wait_recv()
        values = back_held.reshape(chips * slots, PIECE)
        line_at = lax.broadcasted_iota(jnp.int32, (256, 128), 0)
        ids = (lax.div(line_at, 16) * 32 + lax.rem(line_at, 16) + 1).astype(F32)
        rows_of = [
            sum(table[2 * (4 * b + i) + core].astype(F32) for i in range(4)) for b in range(chips // 4)
        ]

        def total_of(g, side):
            shift = (g * 512 + side * 16).astype(F32)
            hot = jnp.concatenate([one_hot(ids == row - shift) for row in rows_of], axis=1)
            return mm(hot, values[...], NN)

        def add_up(g, _):
            more = twin_partial[pl.ds(g * 16, 16)].reshape(256, PIECE).astype(F32)
            total = (total_of(g, core) + more).astype(BF)
            for b in range(16):
                to = g * 16 + b
                target = 2 * to + core
                totals[to] = total[b * images : (b + 1) * images]

                @pl.when(target != me)
                def _():
                    remote(totals.at[to], back_arrived.at[mine], total_send, total_sem, target).start()

                @pl.when(target == me)
                def _():
                    pltpu.make_async_copy(totals.at[to], back_arrived.at[mine], total_sem).start()

            return 0

        lax.fori_loop(0, chips // 16, add_up, 0)

    for t in thirds:
        axis = axis_of(t, 0)
        for d in (1, 2, 3):
            piece = sum_ref.at[4 * t + (spots[axis] + 4 - d) % 4, mine_rows]
            came(t, 2, piece, d).wait()
            start(remote(piece, piece, twin_send.at[t, d], twin_recv.at[t, d], twin))


    pltpu.make_async_copy(back_arrived, back_arrived, total_sem).wait()
    swap = swap_rows(16, images)
    for k in range(3):
        c = slice(k * PIECE, (k + 1) * PIECE)
        stacked = jnp.concatenate([back_arrived[r * 3 + k] for r in range(16)], axis=0)
        query_ref[:, c] = (own_grad[:, c] + mm(swap, stacked, NN)).astype(BF)

    for t in thirds:
        for d in range(4):
            late = sum_ref.at[4 * t + (spots[axis_of(t, 0)] + 4 - d) % 4, twin_rows]
            pltpu.make_async_copy(late, late, twin_recv.at[t, d]).wait()
    for copy in sends:
        copy.wait_send()

    def half_sent(j, _):
        half_copy(j).wait_send()
        return 0

    lax.fori_loop(0, 4 * width // col, half_sent, 0)

    def sent(ref, count, semaphore):
        pltpu.make_async_copy(ref.at[0:count], ref.at[0:count], semaphore).wait()

    for copy in gathers:
        copy.wait_send()

    @pl.when(holding)
    def _():
        swap_copy().wait_send()
        partial_copy().wait_send()
        sent(pieces, HOLDERS - 1, piece_send)
        sent(picked, chips - 1, pick_send)
        sent(back_pieces, HOLDERS - 1, back_send)
        sent(totals, chips - 1, total_send)

    @pl.when(jnp.logical_not(holding))
    def _():
        sent(pieces, HOLDERS, piece_send)
        sent(back_pieces, HOLDERS, back_send)


def pair_losses(lens, ib, need, queries, texts, w, wo, gain, bias, iw, peers):
    own, width = queries.shape
    rows, trows = 3 * own, texts.shape[0]
    images = own // 16
    vmem = pl.BlockSpec(memory_space=pltpu.VMEM)
    smem = pl.BlockSpec(memory_space=pltpu.SMEM)
    shape = jax.ShapeDtypeStruct
    dma = pltpu.SemaphoreType.DMA
    return pl.pallas_call(
        pair_kernel,
        out_shape=(
            shape((rows // 16, 1, 128), F32),
            shape((trows, width), BF),
            shape((own, width), BF),
            shape((12, width, 256), BF),
        ),
        in_specs=[smem, smem] + [vmem] * 3 + [pl.BlockSpec(memory_space=pl.ANY)] * 2 + [vmem] * 3,
        out_specs=(vmem,) * 4,
        scratch_shapes=[
            pltpu.VMEM((rows, width), BF),
            pltpu.VMEM((rows, 3 * width), BF),
            pltpu.VMEM((trows, 2 * width), BF),
            pltpu.VMEM((rows, width), BF),
            pltpu.VMEM((rows, width), F32),
            pltpu.VMEM((rows, width), BF),
            pltpu.VMEM((rows, width), BF),
            pltpu.VMEM((rows, 3 * width), BF),
            pltpu.VMEM((trows, 2 * width), BF),
            pltpu.VMEM((trows, 2 * width), F32),
            pltpu.VMEM((rows, 2 * width), F32),
            pltpu.VMEM((own, width), F32),
            pltpu.VMEM((2 * own, width), BF),
            pltpu.VMEM((12, width, 256), BF),
            pltpu.VMEM((peers, 1, 128), jnp.int32),
            pltpu.VMEM((HOLDERS, images, PIECE), BF),
            pltpu.VMEM((2, peers // 2, images, PIECE), BF),
            pltpu.VMEM((peers // 2, 2 * images, PIECE), BF),
            pltpu.VMEM((HOLDERS, 2 * images, PIECE), BF),
            pltpu.VMEM((HOLDERS, 2 * images, PIECE), BF),
            pltpu.VMEM((peers // 2, 2 * images, PIECE), BF),
            pltpu.VMEM((peers // 2, images, PIECE), BF),
            pltpu.VMEM((peers // 2, images, PIECE), BF),
            pltpu.VMEM((peers // 2, images, PIECE), BF),
            pltpu.VMEM((HOLDERS, images, PIECE), BF),
            pltpu.VMEM((12, 384, 256), BF),
            pltpu.VMEM((3, 3, 384, 256), BF),
            pltpu.VMEM((3, 384, 256), BF),
            pltpu.VMEM((3, 3, 96, 256), BF),
            pltpu.VMEM((3, 96, 256), BF),
            pltpu.VMEM((3, 3, 48, 128), BF),
            pltpu.VMEM((width, 3 * width), BF),
            pltpu.VMEM((width, width), BF),
            dma((2,)), dma((13,)), dma((13,)), dma, dma, dma, dma,
            dma, dma, dma, dma, dma, dma, dma, dma,
            dma((12,)), dma((12,)), dma((3, 10)), dma((3, 10)), dma((3, 10)), dma((3, 10)),
            dma((3, 4)), dma((3, 4)),
        ],
        compiler_params=pltpu.CompilerParams(
            vmem_limit_bytes=63 * 1024 * 1024, has_side_effects=True, collective_id=0
        ),
        name="pair_losses",
    )(lens, ib, need, queries, texts, w, wo, gain, bias, iw.T)


def widen_kernel(share, sum_ref, qkv_ref, out_ref):
    for j in range(12):
        block = sum_ref[j].astype(F32) * share
        if j < 9:
            qkv_ref[:, j * 256 : (j + 1) * 256] = block
        else:
            out_ref[:, (j - 9) * 256 : (j - 8) * 256] = block


def widen(sums, share):
    width, part = sums.shape[1], 96
    return pl.pallas_call(
        lambda *refs: widen_kernel(share, *refs),
        grid=(width // part,),
        out_shape=(
            jax.ShapeDtypeStruct((width, 3 * width), F32),
            jax.ShapeDtypeStruct((width, width), F32),
        ),
        in_specs=[pl.BlockSpec((12, part, 256), lambda j: (0, j, 0))],
        out_specs=(
            pl.BlockSpec((part, 3 * width), lambda j: (j, 0)),
            pl.BlockSpec((part, width), lambda j: (j, 0)),
        ),
        name="widen",
    )(sums)


def on_device(
    text_states, text_len, query_states, neg_owner, neg_slot,
    projection_weight, output_weight, ln_gain, ln_bias, itm_weight, itm_bias,
):
    captions, query_rows, width = query_states.shape
    peers = lax.axis_size("dp")
    me = lax.axis_index("dp")
    wanted = (captions * neg_owner + neg_slot + 1).reshape(1, 2 * captions)
    group = jnp.arange(4)[:, None] == me // 2 % 4
    need = jnp.where(group, wanted, 0).reshape(1, 128)
    logits, grad_text, grad_query, sums = pair_losses(
        text_len, itm_bias, need, query_states.reshape(-1, width), text_states.reshape(-1, width),
        projection_weight, output_weight, ln_gain, ln_bias, itm_weight, peers,
    )
    sum_qkv, sum_out = widen(sums, 1.0 / (captions * peers))
    return (
        jnp.concatenate(
            [logits[:captions, 0, :2].reshape(captions, 1, 2), logits[captions:, 0, :2].reshape(captions, 2, 2)],
            axis=1,
        ),
        grad_text.reshape(text_states.shape),
        grad_query.reshape(query_states.shape),
        sum_qkv,
        sum_out,
    )


def solution(mesh):
    rows = P("dp", None, None)
    placed = (rows, P("dp"), rows, P("dp", None), P("dp", None)) + (P(),) * 6
    return jax.shard_map(
        on_device, mesh=mesh, in_specs=placed, out_specs=(rows, rows, rows, P(), P()), check_vma=False
    )
```

```python
import math
import jax
import jax.numpy as jnp
from jax import lax
from jax.experimental import pallas as pl
from jax.experimental.pallas import tpu as pltpu
from jax.sharding import PartitionSpec as P

F32 = jnp.float32
BF = jnp.bfloat16
NN = (((1,), (0,)), ((), ()))
NT = (((1,), (1,)), ((), ()))
TN = (((0,), (0,)), ((), ()))


def mm(a, b, dims):
    return lax.dot_general(a, b, dims, preferred_element_type=F32)


HOLDERS = 48
PIECE = 256
MESH = pl.DeviceIdType.MESH


def place():
    me = lax.axis_index("dp")
    return me, me // 32, (me // 8) % 4, (me // 2) % 4, me % 2


def device_at(z, y, x, core):
    return ((z * 4 + y) * 4 + x) * 2 + core


def holder(piece, core):
    line, k = piece // 3, piece % 3
    z, y = line // 4, line % 4
    return device_at(z, y, (k + 8 - y - z) % 4, core)


def held_piece():
    me, z, y, x, core = place()
    k = (x + y + z) % 4
    return (z * 4 + y) * 3 + k, k < 3


def one_hot(mask):
    return jnp.where(mask, 1.0, 0.0).astype(BF)


def swap_rows(outer, inner):
    n = outer * inner
    to = lax.broadcasted_iota(jnp.int32, (n, n), 0)
    source = lax.broadcasted_iota(jnp.int32, (n, n), 1)
    return one_hot(source == lax.rem(to, outer) * inner + lax.div(to, outer))


def pair_kernel(
    lens, ibias, need_ref, q_ref, t_ref, w_hbm, wo_hbm, gain_ref, bias_ref, iw_ref,
    logits_ref, gtext_ref, query_ref, sum_ref,
    x, qkv, tkv, ctx, gh, ga, gc, gqkv, gt, gt_own, prob, own_grad, back, grads,
    table, pieces, held, picked, arrived, back_pieces, back_held, partial, twin_partial,
    totals, back_arrived,
    half_in, in1, sum1, in2, sum2, in3,
    w_ref, wo_ref, load_sem, index_send, index_sem, swap_send, swap_recv,
    partial_send, partial_recv, piece_send, held_sem, pick_send, pick_sem,
    back_send, back_sem, total_send, total_sem,
    half_send, half_recv, s_send, s_recv, a_send, a_recv, twin_send, twin_recv,
):
    rows, width = x.shape
    me, z, y, pos_x, core = place()
    mine, holding = held_piece()
    spots = (pos_x, y, z)
    chips, images = held.shape[1], held.shape[2]
    chip = me // 2
    slots = arrived.shape[1]
    pairs_of_heads = width // 128
    unit = 64
    own = q_ref.shape[0]
    scale = 1.0 / math.sqrt(64.0)
    col = 256
    thirds = range(3)

    def along(axis, step):
        at = [pos_x, y, z]
        at[axis] = (at[axis] + step) % 4
        return device_at(at[2], at[1], at[0], core)

    def axis_of(t, stage):
        return (t + stage) % 3

    twin = me + 1 - 2 * core
    mine_rows = pl.ds(pl.multiple_of(core * 384, 128), 384)
    twin_rows = pl.ds(pl.multiple_of(384 - core * 384, 128), 384)

    def remote(source, target, send, recv, device):
        return pltpu.make_async_remote_copy(
            src_ref=source, dst_ref=target, send_sem=send, recv_sem=recv,
            device_id=(device,), device_id_type=MESH)

    barrier = pltpu.get_barrier_semaphore()

    def greet(device):
        pl.semaphore_signal(barrier, inc=1, device_id=(device,), device_id_type=MESH)

    line = me - me % 8
    for d in range(1, 8):
        greet(line + (me + d) % 8)
    for axis in (1, 2):
        for d in (1, 2, 3):
            greet(along(axis, d))

    w_copy = pltpu.make_async_copy(w_hbm, w_ref, load_sem.at[0])
    wo_copy = pltpu.make_async_copy(wo_hbm, wo_ref, load_sem.at[1])
    w_copy.start()
    wo_copy.start()
    swapped = mm(swap_rows(images, 16), q_ref[...], NN).astype(BF)
    for r in range(16):
        for k in range(3):
            pieces[r * 3 + k] = swapped[r * images : (r + 1) * images, k * PIECE : (k + 1) * PIECE]
    table[me] = need_ref[...]
    pl.semaphore_wait(barrier, 13)

    gathers = []

    def gather(rows, device, number):
        copy = remote(table.at[rows], table.at[rows], index_send.at[number], index_sem.at[number], device)
        copy.start()
        gathers.append(copy)

    def gathered(rows, number):
        pltpu.make_async_copy(table.at[rows], table.at[rows], index_sem.at[number]).wait()

    def tkv_step(j, _):
        c = pl.ds(pl.multiple_of(j * col, col), col)
        cw = pl.ds(pl.multiple_of(j * col + width, col), col)
        tkv[:, c] = mm(t_ref[...], w_ref[:, cw], NN).astype(BF)
        return 0

    def own_step(j, _):
        c = pl.ds(pl.multiple_of(j * col, col), col)
        qkv[0:own, c] = mm(q_ref[...], w_ref[:, c], NN).astype(BF)
        return 0

    for d in range(1, 8):
        gather(pl.ds(me, 1), line + (me + d) % 8, d - 1)
    w_copy.wait()
    lax.fori_loop(0, 6, tkv_step, 0)
    for d in range(1, 8):
        gathered(pl.ds(line + (me + 8 - d) % 8, 1), d - 1)
    for d in (1, 2, 3):
        gather(pl.ds(line, 8), along(1, d), 6 + d)
    lax.fori_loop(0, 5, own_step, 0)
    for d in (1, 2, 3):
        gathered(pl.ds((z * 4 + (y + 4 - d) % 4) * 8, 8), 6 + d)
    for d in (1, 2, 3):
        gather(pl.ds(z * 32, 32), along(2, d), 9 + d)
    lax.fori_loop(5, 9, own_step, 0)
    for d in (1, 2, 3):
        gathered(pl.ds(((z + 4 - d) % 4) * 32, 32), 9 + d)

    def spread(i, _):
        piece = (i + me) % HOLDERS
        target = holder(piece, core)

        @pl.when(target != me)
        def _():
            remote(pieces.at[piece], held.at[core, chip], piece_send, held_sem, target).start()

        @pl.when(target == me)
        def _():
            pltpu.make_async_copy(pieces.at[piece], held.at[core, chip], held_sem).start()

        return 0

    lax.fori_loop(0, HOLDERS, spread, 0)
    other = 1 - core

    def swap_copy():
        return remote(held.at[core], held.at[core], swap_send, swap_recv, twin)

    lane = lax.broadcasted_iota(jnp.int32, (1, 128), 1)
    low = lane < 64

    def by_head(a):
        zero = jnp.zeros_like(a)
        return jnp.concatenate([jnp.where(low, a, zero), jnp.where(low, zero, a)], axis=0)

    def spans(negative, u):
        if negative:
            return pl.ds(pl.multiple_of(own + u * unit, 64), unit), pl.ds(pl.multiple_of(u * 32, 32), 32)
        at = pl.ds(pl.multiple_of(u * unit, 64), unit)
        return at, at

    def keys_of(negative, u, j, first):
        r, tr = spans(negative, u)
        parts = [
            qkv[r, first + j * 128 : first + (j + 1) * 128],
            tkv[tr, first - width + j * 128 : first - width + (j + 1) * 128],
        ]
        if negative:
            parts.append(jnp.zeros((32, 128), BF))
        return by_head(jnp.concatenate(parts, axis=0))

    def mask_of(negative, u):
        rowi = lax.broadcasted_iota(jnp.int32, (unit, 128), 0)
        lanei = lax.broadcasted_iota(jnp.int32, (unit, 128), 1)
        block = rowi - lax.rem(rowi, 16)
        if negative:
            first = rowi < 32
            start = jnp.where(first, 64, 80)
            live = jnp.where(first, lens[2 * u], lens[2 * u + 1])
        else:
            start = block + 64
            live = jnp.where(
                rowi < 32,
                jnp.where(rowi < 16, lens[4 * u], lens[4 * u + 1]),
                jnp.where(rowi < 48, lens[4 * u + 2], lens[4 * u + 3]),
            )
        return ((lanei >= block) & (lanei < block + 16)) | ((lanei >= start) & (lanei < start + live))

    def forward(negative, v):
        us = (2 * v, 2 * v + 1)
        heads = [(i, j) for i in range(2) for j in range(pairs_of_heads)]
        rs = [spans(negative, u)[0] for u in us]
        valid = [mask_of(negative, u) for u in us]
        scores = [
            mm(qkv[rs[u], j * 128 : (j + 1) * 128], keys_of(negative, us[u], j, width), NT) * scale for u, j in heads
        ]
        probs = []
        for (u, _), s in zip(heads, scores):
            parts = []
            for h in range(2):
                sh = jnp.where(valid[u], s[:, h * 128 : (h + 1) * 128], -1e30)
                e = jnp.exp(sh - jnp.max(sh, axis=-1, keepdims=True))
                parts.append(e * (1.0 / jnp.sum(e, axis=-1, keepdims=True)))
            probs.append(jnp.concatenate(parts, axis=1))
        outs = [mm(p.astype(BF), keys_of(negative, us[u], j, 2 * width), NN) for (u, j), p in zip(heads, probs)]
        for (u, j), p, o in zip(heads, probs, outs):
            prob[rs[u], j * 256 : (j + 1) * 256] = p
            ctx[rs[u], j * 128 : (j + 1) * 128] = o.astype(BF)

    gain = gain_ref[...].reshape(1, -1)
    bias = bias_ref[...].reshape(1, -1)
    gw0 = gain * iw_ref[0:1, :]
    gw1 = gain * iw_ref[1:2, :]
    slope = (gw1 - gw0) * (1.0 / 16.0)
    slope_mean = jnp.mean(slope)
    base0 = jnp.sum(bias * iw_ref[0:1, :]) + ibias[0]
    base1 = jnp.sum(bias * iw_ref[1:2, :]) + ibias[1]
    part = 256
    tails = part // 16

    def tail(negative, m):
        first = m * part
        r = pl.ds(pl.multiple_of(first, 256), part)
        h = x[r, :].astype(F32) + mm(ctx[r, :], wo_ref[...], NN)
        center = h - jnp.mean(h, axis=-1, keepdims=True)
        spread = jnp.mean(center * center, axis=-1, keepdims=True)
        rstd = lax.rsqrt(spread + 1e-6)
        xhat = center * rstd
        a0 = jnp.sum(xhat * gw0, axis=-1, keepdims=True)
        a1 = jnp.sum(xhat * gw1, axis=-1, keepdims=True)
        l0 = jnp.mean(a0.reshape(tails, 16, 1), axis=1, keepdims=True) + base0
        l1 = jnp.mean(a1.reshape(tails, 16, 1), axis=1, keepdims=True) + base1
        sign = 1.0 if negative else -1.0
        g1 = sign / (1.0 + jnp.exp(-sign * (l1 - l0)))
        g1 = jnp.broadcast_to(g1, (tails, 16, 1)).reshape(part, 1)
        moved = (a1 - a0) * (1.0 / (16.0 * width))
        g = (rstd * g1) * ((slope - slope_mean) - xhat * moved)
        gh[r, :] = g
        low_g = g.astype(BF)
        ga[r, :] = low_g
        gc[r, :] = mm(low_g, wo_ref[...], NT).astype(BF)
        both = jnp.where(lax.broadcasted_iota(jnp.int32, (tails, 1, 128), 2) == 0, l0, l1)
        logits_ref[pl.ds(m * tails, tails)] = both

    def backward(negative, v):
        us = (2 * v, 2 * v + 1)
        heads = [(i, j) for i in range(2) for j in range(pairs_of_heads)]
        rs = [spans(negative, u)[0] for u in us]
        trs = [spans(negative, u)[1] for u in us]
        cols = [slice(j * 128, (j + 1) * 128) for _, j in heads]
        gps = [mm(gc[rs[u], c], keys_of(negative, us[u], j, 2 * width), NT) for (u, j), c in zip(heads, cols)]
        both = []
        for (u, j), gp in zip(heads, gps):
            p = prob[rs[u], j * 256 : (j + 1) * 256]
            gs, lows = [], []
            for h in range(2):
                ph = p[:, h * 128 : (h + 1) * 128]
                gph = gp[:, h * 128 : (h + 1) * 128]
                mean = jnp.sum(gph * ph, axis=-1, keepdims=True)
                gs.append((ph * (gph - mean) * scale).astype(BF))
                lows.append(ph.astype(BF))
            both.append((gs, lows))
        gqs = [
            mm(jnp.concatenate(gs, axis=1), keys_of(negative, us[u], j, width), NN)
            for (u, j), (gs, _) in zip(heads, both)
        ]
        gks = [
            mm(jnp.concatenate(gs, axis=0), by_head(qkv[rs[u], c]), TN)
            for (u, _), c, (gs, _) in zip(heads, cols, both)
        ]
        gvs = [
            mm(jnp.concatenate(lows, axis=0), by_head(gc[rs[u], c]), TN)
            for (u, _), c, (_, lows) in zip(heads, cols, both)
        ]
        for (u, j), c, gq, gk, gv in zip(heads, cols, gqs, gks, gvs):
            r, tr = rs[u], trs[u]
            cv = slice(width + j * 128, width + (j + 1) * 128)
            gqkv[r, c] = gq.astype(BF)
            gqkv[r, cv] = gk[:64].astype(BF)
            gqkv[r, 2 * width + j * 128 : 2 * width + (j + 1) * 128] = gv[:64].astype(BF)
            if negative:
                gt[tr, c] = (gk[64:96] + gt_own[tr, c]).astype(BF)
                gt[tr, cv] = (gv[64:96] + gt_own[tr, cv]).astype(BF)
            else:
                gt_own[tr, c] = gk[64:]
                gt_own[tr, cv] = gv[64:]

    def loop(first, last, step):
        def body(i, _):
            step(i)
            return 0

        lax.fori_loop(first, last, body, 0)

    def to_rows(m):
        r = pl.ds(pl.multiple_of(m * part, 256), part)
        return mm(gqkv[r, :], w_ref[...], NT) + gh[r, :]

    x[0:own, :] = q_ref[...]
    loop(0, own // (2 * unit), lambda v: forward(False, v))

    @pl.when(holding)
    def _():
        pltpu.make_async_copy(held.at[core], held.at[core], held_sem).wait()
        swap_copy().start()
        lanes = lax.broadcasted_iota(jnp.int32, (slots, 128), 1)
        lines = lax.broadcasted_iota(jnp.int32, (slots, 128), 0)
        spot = lax.broadcasted_iota(jnp.int32, (1, 2048), 1)
        side, rest = lax.div(spot, 1024), lax.rem(spot, 1024)
        ids = ((lax.div(rest, 16) * 2 + side) * 16 + lax.rem(rest, 16) + 1).astype(F32)
        values = held.reshape(2048, PIECE)
        pltpu.make_async_copy(held.at[other], held.at[other], swap_recv).wait()

        def pick(g, _):
            columns = []
            for b in range(8):
                row = table[2 * (g * 8 + b) + core].astype(F32)
                eye = lanes == lines + 32 * (b % 4)
                columns.append(jnp.sum(jnp.where(eye, row, 0.0), axis=-1, keepdims=True))
            hot = one_hot(jnp.concatenate(columns, axis=0) == ids)
            chosen = mm(hot, values[...], NN).astype(BF)
            for b in range(8):
                to = g * 8 + b
                target = 2 * to + core
                picked[to] = chosen[b * slots : (b + 1) * slots]

                @pl.when(target != me)
                def _():
                    remote(picked.at[to], arrived.at[mine], pick_send, pick_sem, target).start()

                @pl.when(target == me)
                def _():
                    pltpu.make_async_copy(picked.at[to], arrived.at[mine], pick_sem).start()

            return 0

        lax.fori_loop(0, chips // 8, pick, 0)

    wo_copy.wait()
    loop(0, own // part, lambda m: tail(False, m))
    loop(0, own // (2 * unit), lambda v: backward(False, v))
    own_grad[...] = to_rows(0)

    swap = swap_rows(16, slots)
    pltpu.make_async_copy(arrived, arrived, pick_sem).wait()
    for k in range(3):
        c = slice(k * PIECE, (k + 1) * PIECE)
        stacked = jnp.concatenate([arrived[r * 3 + k] for r in range(16)], axis=0)
        x[own:rows, c] = mm(swap, stacked, NN).astype(BF)

    def negative_step(j):
        c = pl.ds(pl.multiple_of(j * col, col), col)
        qkv[own:rows, c] = mm(x[own:rows, :], w_ref[:, c], NN).astype(BF)

    loop(0, 3 * width // col, negative_step)
    loop(0, (rows - own) // (2 * unit), lambda v: forward(True, v))
    loop(own // part, rows // part, lambda m: tail(True, m))
    loop(0, (rows - own) // (2 * unit), lambda v: backward(True, v))

    def negative_rows(m):
        back[pl.ds(pl.multiple_of((m - 1) * part, 256), part), :] = to_rows(m).astype(BF)

    loop(own // part, rows // part, negative_rows)
    swapped = mm(swap_rows(slots, 16), back[...], NN).astype(BF)
    for r in range(16):
        for k in range(3):
            back_pieces[r * 3 + k] = swapped[r * slots : (r + 1) * slots, k * PIECE : (k + 1) * PIECE]

    def spread_back(i, _):
        piece = (i + me) % HOLDERS
        target = holder(piece, core)

        @pl.when(target != me)
        def _():
            remote(back_pieces.at[piece], back_held.at[chip], back_send, back_sem, target).start()

        @pl.when(target == me)
        def _():
            pltpu.make_async_copy(back_pieces.at[piece], back_held.at[chip], back_sem).start()

        return 0

    lax.fori_loop(0, HOLDERS, spread_back, 0)

    def half_copy(j):
        return remote(grads.at[j, twin_rows], half_in.at[j], half_send.at[j], half_recv.at[j], twin)

    def weight_step(j, _):
        c = pl.ds(pl.multiple_of(j * col, col), col)
        grads[j] = mm(x[...], gqkv[:, c], TN).astype(BF)
        half_copy(j).start()
        return 0

    lax.fori_loop(0, width // col, weight_step, 0)

    def weight_text_step(j, _):
        c = pl.ds(pl.multiple_of(j * col, col), col)
        ct = pl.ds(pl.multiple_of(j * col - width, col), col)
        grads[j] = (mm(x[...], gqkv[:, c], TN) + mm(t_ref[...], gt[:, ct], TN)).astype(BF)
        half_copy(j).start()
        return 0

    lax.fori_loop(width // col, 3 * width // col, weight_text_step, 0)

    def out_step(j, _):
        c = pl.ds(pl.multiple_of(j * col - 3 * width, col), col)
        grads[j] = mm(ctx[...], ga[:, c], TN).astype(BF)
        half_copy(j).start()
        return 0

    lax.fori_loop(3 * width // col, 4 * width // col, out_step, 0)

    sends = []

    def start(copy):
        copy.start()
        sends.append(copy)

    one = {}
    for t in thirds:
        axis = axis_of(t, 0)

        def add_half(k, _, t=t):
            half_copy(4 * t + k).wait_recv()
            own = grads[4 * t + k, mine_rows, :].astype(F32)
            half_in[4 * t + k] = (own + half_in[4 * t + k].astype(F32)).astype(BF)
            return 0

        lax.fori_loop(0, 4, add_half, 0)
        for d in (1, 2, 3):
            to = (spots[axis] + d) % 4
            one[t, d] = remote(half_in.at[4 * t + to], in1.at[t, d - 1],
                               s_send.at[t, d], s_recv.at[t, d], along(axis, d))
            start(one[t, d])

    def partial_copy():
        return remote(partial, twin_partial, partial_send, partial_recv, twin)

    @pl.when(holding)
    def _():
        pltpu.make_async_copy(back_held, back_held, back_sem).wait()
        values = back_held.reshape(chips * slots, PIECE)
        line_at = lax.broadcasted_iota(jnp.int32, (256, 128), 0)
        ids = (lax.div(line_at, 16) * 32 + lax.rem(line_at, 16) + 1).astype(F32)
        rows_of = [
            sum(table[2 * (4 * b + i) + core].astype(F32) for i in range(4)) for b in range(chips // 4)
        ]

        def total_of(g, side):
            shift = (g * 512 + side * 16).astype(F32)
            hot = jnp.concatenate([one_hot(ids == row - shift) for row in rows_of], axis=1)
            return mm(hot, values[...], NN)

        def for_twin(g, _):
            total = total_of(g, other).astype(BF)
            for b in range(16):
                partial[g * 16 + b] = total[b * images : (b + 1) * images]
            return 0

        lax.fori_loop(0, chips // 16, for_twin, 0)
        partial_copy().start()

    gtext_ref[...] = mm(gt[...], w_ref[:, width:], NT).astype(BF)

    two = {}
    for t in thirds:
        axis, after = axis_of(t, 0), axis_of(t, 1)
        for d in (1, 2, 3):
            one[t, d].wait_recv()
        total = half_in[4 * t + spots[axis]].astype(F32)
        for d in range(3):
            total += in1[t, d].astype(F32)
        sum1[t] = total.astype(BF)
        for d in (1, 2, 3):
            to = (spots[after] + d) % 4
            two[t, d] = remote(sum1.at[t, pl.ds(pl.multiple_of(to * 96, 32), 96)], in2.at[t, d - 1],
                               s_send.at[t, 3 + d], s_recv.at[t, 3 + d], along(after, d))
            start(two[t, d])

    def corner(ref, first, spot):
        rows = pl.ds(pl.multiple_of(first + (spot // 2) * 48, 16), 48)
        return ref.at[rows, pl.ds(pl.multiple_of((spot % 2) * 128, 128), 128)]

    three = {}
    for t in thirds:
        axis, after = axis_of(t, 1), axis_of(t, 2)
        for d in (1, 2, 3):
            two[t, d].wait_recv()
        total = sum1[t, pl.ds(pl.multiple_of(spots[axis] * 96, 32), 96), :].astype(F32)
        for d in range(3):
            total += in2[t, d].astype(F32)
        sum2[t] = total.astype(BF)
        for d in (1, 2, 3):
            to = (spots[after] + d) % 4
            three[t, d] = remote(corner(sum2.at[t], 0, to), in3.at[t, d - 1],
                                 s_send.at[t, 6 + d], s_recv.at[t, 6 + d], along(after, d))
            start(three[t, d])

    last = {}
    for t in thirds:
        axis = axis_of(t, 2)
        for d in (1, 2, 3):
            three[t, d].wait_recv()
        total = corner(sum2.at[t], 0, spots[axis])[...].astype(F32)
        for d in range(3):
            total += in3[t, d].astype(F32)
        block = sum_ref.at[4 * t + spots[axis_of(t, 0)]]
        first = core * 384 + spots[axis_of(t, 1)] * 96
        piece = corner(block, first, spots[axis])
        piece[...] = total.astype(BF)
        for d in (1, 2, 3):
            last[t, d] = remote(piece, piece, a_send.at[t, d], a_recv.at[t, d], along(axis, d))
            start(last[t, d])

    def came(t, stage, ref, d):
        return pltpu.make_async_copy(ref, ref, a_recv.at[t, stage * 3 + d])

    for t in thirds:
        axis = axis_of(t, 1)
        block = sum_ref.at[4 * t + spots[axis_of(t, 0)]]
        first = core * 384 + spots[axis] * 96
        for d in (1, 2, 3):
            came(t, 0, corner(block, first, (spots[axis_of(t, 2)] + 4 - d) % 4), d).wait()
        piece = block.at[pl.ds(pl.multiple_of(first, 32), 96)]
        for d in (1, 2, 3):
            start(remote(piece, piece, a_send.at[t, 3 + d], a_recv.at[t, 3 + d], along(axis, d)))

    for t in thirds:
        axis = axis_of(t, 0)
        block = sum_ref.at[4 * t + spots[axis]]
        for d in (1, 2, 3):
            spot = (spots[axis_of(t, 1)] + 4 - d) % 4
            came(t, 1, block.at[pl.ds(pl.multiple_of(core * 384 + spot * 96, 32), 96)], d).wait()
        piece = block.at[mine_rows]
        start(remote(piece, piece, twin_send.at[t, 0], twin_recv.at[t, 0], twin))
        for d in (1, 2, 3):
            start(remote(piece, piece, a_send.at[t, 6 + d], a_recv.at[t, 6 + d], along(axis, d)))

    @pl.when(holding)
    def _():
        partial_copy().wait_recv()
        values = back_held.reshape(chips * slots, PIECE)
        line_at = lax.broadcasted_iota(jnp.int32, (256, 128), 0)
        ids = (lax.div(line_at, 16) * 32 + lax.rem(line_at, 16) + 1).astype(F32)
        rows_of = [
            sum(table[2 * (4 * b + i) + core].astype(F32) for i in range(4)) for b in range(chips // 4)
        ]

        def total_of(g, side):
            shift = (g * 512 + side * 16).astype(F32)
            hot = jnp.concatenate([one_hot(ids == row - shift) for row in rows_of], axis=1)
            return mm(hot, values[...], NN)

        def add_up(g, _):
            more = twin_partial[pl.ds(g * 16, 16)].reshape(256, PIECE).astype(F32)
            total = (total_of(g, core) + more).astype(BF)
            for b in range(16):
                to = g * 16 + b
                target = 2 * to + core
                totals[to] = total[b * images : (b + 1) * images]

                @pl.when(target != me)
                def _():
                    remote(totals.at[to], back_arrived.at[mine], total_send, total_sem, target).start()

                @pl.when(target == me)
                def _():
                    pltpu.make_async_copy(totals.at[to], back_arrived.at[mine], total_sem).start()

            return 0

        lax.fori_loop(0, chips // 16, add_up, 0)

    for t in thirds:
        axis = axis_of(t, 0)
        for d in (1, 2, 3):
            piece = sum_ref.at[4 * t + (spots[axis] + 4 - d) % 4, mine_rows]
            came(t, 2, piece, d).wait()
            start(remote(piece, piece, twin_send.at[t, d], twin_recv.at[t, d], twin))


    pltpu.make_async_copy(back_arrived, back_arrived, total_sem).wait()
    swap = swap_rows(16, images)
    for k in range(3):
        c = slice(k * PIECE, (k + 1) * PIECE)
        stacked = jnp.concatenate([back_arrived[r * 3 + k] for r in range(16)], axis=0)
        query_ref[:, c] = (own_grad[:, c] + mm(swap, stacked, NN)).astype(BF)

    for t in thirds:
        for d in range(4):
            late = sum_ref.at[4 * t + (spots[axis_of(t, 0)] + 4 - d) % 4, twin_rows]
            pltpu.make_async_copy(late, late, twin_recv.at[t, d]).wait()
    for copy in sends:
        copy.wait_send()

    def half_sent(j, _):
        half_copy(j).wait_send()
        return 0

    lax.fori_loop(0, 4 * width // col, half_sent, 0)

    def sent(ref, count, semaphore):
        pltpu.make_async_copy(ref.at[0:count], ref.at[0:count], semaphore).wait()

    for copy in gathers:
        copy.wait_send()

    @pl.when(holding)
    def _():
        swap_copy().wait_send()
        partial_copy().wait_send()
        sent(pieces, HOLDERS - 1, piece_send)
        sent(picked, chips - 1, pick_send)
        sent(back_pieces, HOLDERS - 1, back_send)
        sent(totals, chips - 1, total_send)

    @pl.when(jnp.logical_not(holding))
    def _():
        sent(pieces, HOLDERS, piece_send)
        sent(back_pieces, HOLDERS, back_send)


def pair_losses(lens, ib, need, queries, texts, w, wo, gain, bias, iw, peers):
    own, width = queries.shape
    rows, trows = 3 * own, texts.shape[0]
    images = own // 16
    vmem = pl.BlockSpec(memory_space=pltpu.VMEM)
    smem = pl.BlockSpec(memory_space=pltpu.SMEM)
    shape = jax.ShapeDtypeStruct
    dma = pltpu.SemaphoreType.DMA
    return pl.pallas_call(
        pair_kernel,
        out_shape=(
            shape((rows // 16, 1, 128), F32),
            shape((trows, width), BF),
            shape((own, width), BF),
            shape((12, width, 256), BF),
        ),
        in_specs=[smem, smem] + [vmem] * 3 + [pl.BlockSpec(memory_space=pl.ANY)] * 2 + [vmem] * 3,
        out_specs=(vmem,) * 4,
        scratch_shapes=[
            pltpu.VMEM((rows, width), BF),
            pltpu.VMEM((rows, 3 * width), BF),
            pltpu.VMEM((trows, 2 * width), BF),
            pltpu.VMEM((rows, width), BF),
            pltpu.VMEM((rows, width), F32),
            pltpu.VMEM((rows, width), BF),
            pltpu.VMEM((rows, width), BF),
            pltpu.VMEM((rows, 3 * width), BF),
            pltpu.VMEM((trows, 2 * width), BF),
            pltpu.VMEM((trows, 2 * width), F32),
            pltpu.VMEM((rows, 2 * width), F32),
            pltpu.VMEM((own, width), F32),
            pltpu.VMEM((2 * own, width), BF),
            pltpu.VMEM((12, width, 256), BF),
            pltpu.VMEM((peers, 1, 128), jnp.int32),
            pltpu.VMEM((HOLDERS, images, PIECE), BF),
            pltpu.VMEM((2, peers // 2, images, PIECE), BF),
            pltpu.VMEM((peers // 2, 2 * images, PIECE), BF),
            pltpu.VMEM((HOLDERS, 2 * images, PIECE), BF),
            pltpu.VMEM((HOLDERS, 2 * images, PIECE), BF),
            pltpu.VMEM((peers // 2, 2 * images, PIECE), BF),
            pltpu.VMEM((peers // 2, images, PIECE), BF),
            pltpu.VMEM((peers // 2, images, PIECE), BF),
            pltpu.VMEM((peers // 2, images, PIECE), BF),
            pltpu.VMEM((HOLDERS, images, PIECE), BF),
            pltpu.VMEM((12, 384, 256), BF),
            pltpu.VMEM((3, 3, 384, 256), BF),
            pltpu.VMEM((3, 384, 256), BF),
            pltpu.VMEM((3, 3, 96, 256), BF),
            pltpu.VMEM((3, 96, 256), BF),
            pltpu.VMEM((3, 3, 48, 128), BF),
            pltpu.VMEM((width, 3 * width), BF),
            pltpu.VMEM((width, width), BF),
            dma((2,)), dma((13,)), dma((13,)), dma, dma, dma, dma,
            dma, dma, dma, dma, dma, dma, dma, dma,
            dma((12,)), dma((12,)), dma((3, 10)), dma((3, 10)), dma((3, 10)), dma((3, 10)),
            dma((3, 4)), dma((3, 4)),
        ],
        compiler_params=pltpu.CompilerParams(
            vmem_limit_bytes=63 * 1024 * 1024, has_side_effects=True, collective_id=0
        ),
        name="pair_losses",
    )(lens, ib, need, queries, texts, w, wo, gain, bias, iw.T)


def widen_kernel(share, sum_ref, qkv_ref, out_ref):
    for j in range(12):
        block = sum_ref[j].astype(F32) * share
        if j < 9:
            qkv_ref[:, j * 256 : (j + 1) * 256] = block
        else:
            out_ref[:, (j - 9) * 256 : (j - 8) * 256] = block


def widen(sums, share):
    width, part = sums.shape[1], 192
    return pl.pallas_call(
        lambda *refs: widen_kernel(share, *refs),
        grid=(width // part,),
        out_shape=(
            jax.ShapeDtypeStruct((width, 3 * width), F32),
            jax.ShapeDtypeStruct((width, width), F32),
        ),
        in_specs=[pl.BlockSpec((12, part, 256), lambda j: (0, j, 0))],
        out_specs=(
            pl.BlockSpec((part, 3 * width), lambda j: (j, 0)),
            pl.BlockSpec((part, width), lambda j: (j, 0)),
        ),
        compiler_params=pltpu.CompilerParams(vmem_limit_bytes=32 * 1024 * 1024),
        name="widen",
    )(sums)


def on_device(
    text_states, text_len, query_states, neg_owner, neg_slot,
    projection_weight, output_weight, ln_gain, ln_bias, itm_weight, itm_bias,
):
    captions, query_rows, width = query_states.shape
    peers = lax.axis_size("dp")
    me = lax.axis_index("dp")
    wanted = (captions * neg_owner + neg_slot + 1).reshape(1, 2 * captions)
    group = jnp.arange(4)[:, None] == me // 2 % 4
    need = jnp.where(group, wanted, 0).reshape(1, 128)
    logits, grad_text, grad_query, sums = pair_losses(
        text_len, itm_bias, need, query_states.reshape(-1, width), text_states.reshape(-1, width),
        projection_weight, output_weight, ln_gain, ln_bias, itm_weight, peers,
    )
    sum_qkv, sum_out = widen(sums, 1.0 / (captions * peers))
    return (
        jnp.concatenate(
            [logits[:captions, 0, :2].reshape(captions, 1, 2), logits[captions:, 0, :2].reshape(captions, 2, 2)],
            axis=1,
        ),
        grad_text.reshape(text_states.shape),
        grad_query.reshape(query_states.shape),
        sum_qkv,
        sum_out,
    )


def solution(mesh):
    rows = P("dp", None, None)
    placed = (rows, P("dp"), rows, P("dp", None), P("dp", None)) + (P(),) * 6
    return jax.shard_map(
        on_device, mesh=mesh, in_specs=placed, out_specs=(rows, rows, rows, P(), P()), check_vma=False
    )
```
